256 devices in a mesh: trk: 32 (over x, y, z_hi), frm: 8 (over z_lo, core).
Axes of the slice: x: 4, y: 4, z: 8 (z_hi: 2, z_lo: 4; z = z_hi * 4 + z_lo), core: 2. Of those that a mesh axis runs over, the one named last changes fastest.
Arguments:
- tokens: bfloat16 [2048, 128, 384], P('trk', 'frm'), may hold values from -6 to 6
- visible: int32 [2048, 128], P('trk', 'frm'), may hold values 0 or 1
- virtual: bfloat16 [128, 64, 384], P('frm'), may hold values from -6 to 6
- gains: float32 [7, 384], replicated, may hold values from 0.1 to 1.9
- w_time_qkv: bfloat16 [384, 1152], replicated, may hold values from -9.3386796 to 9.3386796
- w_time_o: bfloat16 [384, 384], replicated, may hold values from -0.3125 to 0.3125
- w_read_q: bfloat16 [384, 384], replicated, may hold values from -0.30618622 to 0.30618622
- w_read_kv: bfloat16 [384, 768], replicated, may hold values from -18.473235143489802 to 18.473235143489802
- w_read_o: bfloat16 [384, 384], replicated, may hold values from -0.3125 to 0.3125
- w_write_q: bfloat16 [384, 384], replicated, may hold values from -0.3125 to 0.3125
- w_write_kv: bfloat16 [384, 768], replicated, may hold values from -0.3125 to 0.3125
- w_write_o: bfloat16 [384, 384], replicated, may hold values from -0.3125 to 0.3125
- w_up: bfloat16 [384, 1536], replicated, may hold values from -0.3125 to 0.3125
- w_down: bfloat16 [1536, 384], replicated, may hold values from -0.15625 to 0.15625
- v_up: bfloat16 [384, 1536], replicated, may hold values from -0.3125 to 0.3125
- v_down: bfloat16 [1536, 384], replicated, may hold values from -0.15625 to 0.15625
Outputs:
- track_out: bfloat16 [2048, 128, 384], P('trk', 'frm')
- virt_out: bfloat16 [128, 64, 384], P('frm')
The draws below stay inside these ranges and needn't reach their ends.
All inputs are finite; a program needn't handle non-finite values. No bound on the sum of `visible` on one device may be relied on, other than what follows from the above.
Results may differ from the reference program's by a relative error of at most 0.025.
The reference program's roundings to bfloat16 on the way count: a program that leaves them out, or rounds other values in their place, can miss the bound.
Values may be sent and summed in bfloat16 or wider, within the bound.
A program may use at most 128 MiB of HBM per device.

```python
import math
import jax
import jax.numpy as jnp
from jax import lax

D = 384
HEADS = 8
HID = 1536
V = 64
TRACKS = 2048
FRAMES = 128


def draw_w_time_qkv(key, part):
    key = jax.random.fold_in(key, 11)
    first_key = jax.random.fold_in(key, 0)
    base = jnp.clip(jax.random.normal(first_key, (D, 3 * D), jnp.float32), -6.0, 6.0) * D ** (-0.5)
    return base.astype(jnp.bfloat16)


def read_query_base(key):
    shared_key = jax.random.fold_in(key, 40)
    return jnp.clip(jax.random.normal(shared_key, (D, D), jnp.float32), -6.0, 6.0) * D ** (-0.5)


def draw_w_read_q(key, part):
    shared = read_query_base(key)
    return shared.astype(jnp.bfloat16)


def draw_w_read_kv(key, part):
    key = jax.random.fold_in(key, 23)
    first_key = jax.random.fold_in(key, 0)
    base = jnp.clip(jax.random.normal(first_key, (D, 2 * D), jnp.float32), -6.0, 6.0) * D ** (-0.5)
    return base.astype(jnp.bfloat16)


def plant(drawn, stream_key, least, high):
    longest = drawn.shape.index(max(drawn.shape))
    spots = []
    for shift in (0, 1):
        where = [jax.random.randint(jax.random.fold_in(stream_key, axis), (), 0, length) for axis, length in enumerate(drawn.shape)]
        where[longest] = (where[longest] + shift) % drawn.shape[longest]
        spots.append(tuple(where))
    return drawn.at[spots[0]].set(least).at[spots[1]].set(high)


def block_scale(rng, dims, cuts, least, high):
    def one(dim, parts):
        steps = jax.random.uniform(jax.random.fold_in(jax.random.fold_in(rng, 6), dim), (parts,), jnp.float32, least / len(cuts), high / len(cuts))
        return jnp.repeat(jnp.exp(steps), dims[dim] // parts).reshape((-1,) + (1,) * (len(dims) - dim - 1))

    level = one(*cuts[0])
    for cut in cuts[1:]:
        level = level * one(*cut)
    return level


def gaussian(rng, extent, width, reach, shards=(), dtype=jnp.bfloat16):
    array = jax.random.normal(rng, extent, jnp.float32) * width
    if len(shards) > 0:
        array = block_scale(rng, extent, shards, -0.22, 0.18) * array
    return jnp.clip(array, min=-reach, max=reach).astype(dtype)


def setup_inputs(seed: int = 0) -> dict:
    key_of = jax.random.split(jax.random.key(seed), 17)
    tokens = gaussian(key_of[0], (TRACKS, FRAMES, D), 1.0, 6.0, ((0, 32), (1, 8)))
    visible = plant((jax.random.randint(key_of[1], (TRACKS, FRAMES), 0, 4) < 3).astype(jnp.int32), jax.random.fold_in(key_of[1], 1), 0, 1)
    virtual = gaussian(key_of[2], (FRAMES, V, D), 1.0, 6.0, ((0, 8),))
    gains = jnp.clip(1.0 + 0.18 * jax.random.normal(key_of[3], (7, D), jnp.float32), 0.1, 1.9)
    w_time_qkv = draw_w_time_qkv(jax.random.fold_in(key_of[16], 71), 0)
    w_time_o = gaussian(key_of[5], (D, D), D ** -0.5, 0.3125)
    w_read_q = draw_w_read_q(jax.random.fold_in(key_of[16], 71), 0)
    w_read_kv = draw_w_read_kv(jax.random.fold_in(key_of[16], 71), 0)
    w_read_o = gaussian(key_of[8], (D, D), D ** -0.5, 0.3125)
    w_write_q = gaussian(key_of[9], (D, D), D ** -0.5, 0.3125)
    w_write_kv = gaussian(key_of[10], (D, 2 * D), D ** -0.5, 0.3125)
    w_write_o = gaussian(key_of[11], (D, D), D ** -0.5, 0.3125)
    w_up = gaussian(key_of[12], (D, HID), D ** -0.5, 0.3125)
    w_down = gaussian(key_of[13], (HID, D), HID ** -0.5, 0.15625)
    v_up = gaussian(key_of[14], (D, HID), D ** -0.5, 0.3125)
    v_down = gaussian(key_of[15], (HID, D), HID ** -0.5, 0.15625)
    return dict(tokens=tokens, visible=visible, virtual=virtual, gains=gains, w_time_qkv=w_time_qkv, w_time_o=w_time_o, w_read_q=w_read_q, w_read_kv=w_read_kv, w_read_o=w_read_o, w_write_q=w_write_q, w_write_kv=w_write_kv, w_write_o=w_write_o, w_up=w_up, w_down=w_down, v_up=v_up, v_down=v_down)


penalty = 4.0
epsilon = 1e-05

def layer_norm(inputs, gain_row):
    values = inputs.astype(jnp.float32)
    center = values - lax.optimization_barrier(jnp.mean(values, axis=-1, keepdims=True))
    spread = lax.optimization_barrier(jnp.mean(center * center, axis=-1, keepdims=True))
    return center * lax.rsqrt(spread + epsilon) * gain_row

def attend_heads(queries, keys, values, key_bias):
    batch, rows_q, model_width = queries.shape
    rows_k = keys.shape[1]
    head_size = model_width // HEADS
    qheads = queries.reshape(batch, rows_q, HEADS, head_size).astype(jnp.float32)
    kheads = keys.reshape(batch, rows_k, HEADS, head_size).astype(jnp.float32)
    vheads = values.reshape(batch, rows_k, HEADS, head_size).astype(jnp.float32)
    scores = jnp.einsum('bqhd,bkhd->bhqk', qheads, kheads) / math.sqrt(head_size)
    if key_bias is not None:
        scores = scores + key_bias.astype(jnp.float32)[:, None, None, :]
    peak = lax.optimization_barrier(jnp.max(scores, axis=-1, keepdims=True))
    expos = jnp.exp(scores - peak)
    totals = lax.optimization_barrier(jnp.sum(expos, axis=-1))
    rounded = lax.optimization_barrier(expos.astype(jnp.bfloat16)).astype(jnp.float32)
    numer = jnp.einsum('bhqk,bkhd->bqhd', rounded, vheads)
    output = numer / jnp.transpose(totals, (0, 2, 1))[..., None]
    return output.reshape(batch, rows_q, model_width).astype(jnp.bfloat16)

def feed_forward(normed, w_first, w_second):
    middle = jax.nn.gelu(jnp.dot(normed, w_first, preferred_element_type=jnp.float32), approximate=True)
    return jnp.dot(middle.astype(jnp.bfloat16), w_second, preferred_element_type=jnp.float32)

def reference(tokens, visible, virtual, gains, w_time_qkv, w_time_o, w_read_q, w_read_kv, w_read_o, w_write_q, w_write_kv, w_write_o, w_up, w_down, v_up, v_down):
    visible_bias = (visible.astype(jnp.float32) - 1.0) * penalty
    block = math.gcd(TRACKS, 64)
    count = TRACKS // block

    def first_section(pieces):
        rows, row_bias = pieces
        normed = layer_norm(rows, gains[0]).astype(jnp.bfloat16)
        triple = jnp.dot(normed, w_time_qkv, preferred_element_type=jnp.float32).astype(jnp.bfloat16)
        attended = attend_heads(triple[..., :D], triple[..., D:2 * D], triple[..., 2 * D:], row_bias)
        time_out = jnp.dot(attended, w_time_o, preferred_element_type=jnp.float32).astype(jnp.bfloat16)
        first = (rows.astype(jnp.float32) + time_out.astype(jnp.float32)).astype(jnp.bfloat16)
        normed_two = layer_norm(first, gains[1]).astype(jnp.bfloat16)
        pairs = jnp.dot(normed_two, w_read_kv, preferred_element_type=jnp.float32).astype(jnp.bfloat16)
        return (first, pairs)
    first, pairs = lax.map(first_section, (tokens.reshape(count, block, FRAMES, D), visible_bias.reshape(count, block, FRAMES)))
    first = first.reshape(TRACKS, FRAMES, D)
    pairs = jnp.transpose(pairs.reshape(TRACKS, FRAMES, 2 * D), (1, 0, 2))
    vnormed = layer_norm(virtual, gains[4]).astype(jnp.bfloat16)
    vquery = jnp.dot(vnormed, w_read_q, preferred_element_type=jnp.float32).astype(jnp.bfloat16)

    def read_frame(pieces):
        query_rows, frame_pairs, frame_bias = pieces
        return attend_heads(query_rows[None], frame_pairs[None, :, :D], frame_pairs[None, :, D:], frame_bias[None])[0]
    readout = lax.map(read_frame, (vquery, pairs, jnp.transpose(visible_bias)))
    virt1 = (virtual.astype(jnp.float32) + jnp.dot(readout, w_read_o, preferred_element_type=jnp.float32)).astype(jnp.bfloat16)
    vnormed_two = layer_norm(virt1, gains[5]).astype(jnp.bfloat16)
    virt_out = (virt1.astype(jnp.float32) + feed_forward(vnormed_two, v_up, v_down)).astype(jnp.bfloat16)
    keyed = layer_norm(virt_out, gains[6]).astype(jnp.bfloat16)
    write_pairs = jnp.dot(keyed, w_write_kv, preferred_element_type=jnp.float32).astype(jnp.bfloat16)

    def second_section(rows):
        normed = layer_norm(rows, gains[2]).astype(jnp.bfloat16)
        queries = jnp.dot(normed, w_write_q, preferred_element_type=jnp.float32).astype(jnp.bfloat16)
        attended = attend_heads(jnp.transpose(queries, (1, 0, 2)), write_pairs[..., :D], write_pairs[..., D:], None)
        attended = jnp.transpose(attended, (1, 0, 2))
        second = (rows.astype(jnp.float32) + jnp.dot(attended, w_write_o, preferred_element_type=jnp.float32)).astype(jnp.bfloat16)
        normed_two = layer_norm(second, gains[3]).astype(jnp.bfloat16)
        return (second.astype(jnp.float32) + feed_forward(normed_two, w_up, w_down)).astype(jnp.bfloat16)
    track_out = lax.map(second_section, first.reshape(count, block, FRAMES, D)).reshape(TRACKS, FRAMES, D)
    return (track_out, virt_out)
```

```python
import functools
import math

import jax
import jax.numpy as jnp
from jax import lax
from jax.experimental import pallas as pl
from jax.experimental.pallas import tpu as pltpu
from jax.sharding import PartitionSpec as P

HEADS = 8
HEAD = 48
SLOT = 64
TILE = 128
PAIRS = HEADS // 2
WIDE = HEADS * SLOT
PENALTY = 4.0
EPSILON = 1e-05
SCALE = 1.0 / math.sqrt(HEAD)
MESH = pl.DeviceIdType.MESH
f32 = jnp.float32
bf16 = jnp.bfloat16


def dot(a, b):
    return lax.dot_general(a, b, (((1,), (0,)), ((), ())), preferred_element_type=f32)


def dot_t(a, b):
    return lax.dot_general(a, b, (((1,), (1,)), ((), ())), preferred_element_type=f32)


def unit(x):
    center = x - jnp.mean(x, axis=-1, keepdims=True)
    spread = jnp.mean(center * center, axis=-1, keepdims=True)
    return center * lax.rsqrt(spread + EPSILON)


def gelu(x):
    return jax.nn.gelu(x, approximate=True)


def spread_matrix(rows_are_padded):
    shape = (WIDE, HEADS * HEAD) if rows_are_padded else (HEADS * HEAD, WIDE)
    tight = lax.broadcasted_iota(jnp.int32, shape, 1 if rows_are_padded else 0)
    padded = lax.broadcasted_iota(jnp.int32, shape, 0 if rows_are_padded else 1)
    target = tight
    for h in range(1, HEADS):
        target = target + jnp.where(tight >= HEAD * h, SLOT - HEAD, 0)
    return jnp.where(target == padded, 1.0, 0.0).astype(bf16)


def halves(x, lane):
    zero = jnp.zeros_like(x)
    return jnp.concatenate(
        [jnp.where(lane < SLOT, x, zero), jnp.where(lane < SLOT, zero, x)], axis=0
    )


def lanes(rows):
    return lax.broadcasted_iota(jnp.int32, (rows, TILE), 1)


def slot_lanes(rows):
    lane = lanes(rows)
    return jnp.where(lane < SLOT, lane, lane - SLOT)


def pair_attention(q, k, v, bias):
    lane_k, lane_q = lanes(k.shape[0]), lanes(q.shape[0])
    v = jnp.where(slot_lanes(v.shape[0]) == HEAD, jnp.ones_like(v), v)
    s = dot_t(q, halves(k, lane_k)) * SCALE
    if bias is not None:
        s = s + bias
    low = jnp.full_like(s, -jnp.inf)
    first = jnp.max(jnp.where(lane_q < SLOT, s, low), axis=-1, keepdims=True)
    second = jnp.max(jnp.where(lane_q < SLOT, low, s), axis=-1, keepdims=True)
    peak = jnp.where(lane_q < SLOT, first, second)
    e = jnp.exp(s - peak).astype(bf16)
    return dot(e, halves(v, lane_k)), peak


def with_peak(num, peak):
    place = slot_lanes(num.shape[0])
    high = peak.astype(bf16).astype(f32)
    rest = peak - high
    mid = rest.astype(bf16).astype(f32)
    low = rest - mid
    num = jnp.where(place == HEAD + 1, high, num)
    num = jnp.where(place == HEAD + 2, mid, num)
    num = jnp.where(place == HEAD + 3, low, num)
    return num.astype(bf16)


def over_den(num):
    rows = num.shape[0]
    den = jnp.where(lanes(rows) < SLOT, num[:, HEAD : HEAD + 1], num[:, SLOT + HEAD : SLOT + HEAD + 1])
    return jnp.where(slot_lanes(rows) < HEAD, num / den, 0.0).astype(bf16)


def merge(ref, pair):
    count, rows = ref.shape[0], ref.shape[1]
    part = ref[:, :, pair * TILE : (pair + 1) * TILE]
    flat = part.reshape(count * rows, TILE)
    row = lax.broadcasted_iota(jnp.int32, (TILE, TILE), 0)
    col = lax.broadcasted_iota(jnp.int32, (TILE, TILE), 1)
    same = (row < SLOT) == (col < SLOT)
    place = jnp.where(row < SLOT, row, row - SLOT)
    pick = same & (place > HEAD) & (place < HEAD + 4)
    peaks = dot(flat, jnp.where(pick, 1.0, 0.0).astype(bf16)).reshape(count, rows, TILE)
    peak = jnp.max(peaks, axis=0)
    total = jnp.sum(jnp.exp(peaks - peak[None]) * part.astype(f32), axis=0)
    return total, peak


def kernel(
    dims,
    tokens,
    vis,
    read_bias,
    virtual,
    gains,
    w_time_qkv,
    w_time_o,
    w_read_q,
    w_read_kv,
    w_read_o,
    w_write_q,
    w_write_kv,
    w_write_o,
    w_up,
    w_down,
    v_up,
    v_down,
    track_out,
    virt_out,
    tok,
    x_recv,
    stage,
    y_recv,
    vis_recv,
    time_bias,
    y1t,
    y1,
    virt,
    vq,
    kv2,
    wq,
    part_send,
    part_recv,
    cross,
    vout,
    outt,
    raw,
    r_up,
    r_down,
    r_vup,
    r_vdown,
    p_time_qkv,
    p_time_o,
    p_read_q,
    p_read_kv,
    p_read_o,
    p_write_q,
    p_write_kv,
    p_write_o,
    load_sem,
    own_sem,
    vis_sem,
    tok_sem,
    back_sem,
    part_sem,
    cross_sem,
    gather_sem,
    out_sem,
):
    nfrm, nplane, chunks, per, frames = dims
    trk, me = lax.axis_index("trk"), lax.axis_index("frm")
    spot, half = lax.div(trk, 2), lax.rem(trk, 2)
    width = HEADS * HEAD
    group = min(4, frames)

    def column(k):
        return lax.rem(me + k, nfrm)

    def plane(i):
        return lax.rem(spot + i, nplane)

    weights = (w_time_qkv, w_time_o, w_read_q, w_read_kv, w_read_o, w_write_q, w_write_kv, w_write_o)
    offsets = []
    at = 0
    loads = []
    for n, w in enumerate(weights):
        cols = w.shape[1]
        offsets.append((at, cols))
        loads.append(pltpu.make_async_copy(w, raw.at[:, pl.ds(at, cols)], load_sem.at[n]))
        at += cols
    for w, dst in ((w_up, r_up), (w_down, r_down), (v_up, r_vup), (v_down, r_vdown), (virtual, virt), (tokens, tok)):
        loads.append(pltpu.make_async_copy(w, dst, load_sem.at[len(loads)]))
    own = pltpu.make_async_copy(tokens.at[me], x_recv.at[me], own_sem)

    barrier = pltpu.get_barrier_semaphore()

    def greet_column(k, carry):
        pl.semaphore_signal(barrier, inc=1, device_id=(trk, column(k)), device_id_type=MESH)
        return carry

    def greet_plane(i, carry):
        pl.semaphore_signal(barrier, inc=1, device_id=(plane(i) * 2 + half, me), device_id_type=MESH)
        return carry

    lax.fori_loop(1, nfrm, greet_column, 0)
    lax.fori_loop(1, nplane, greet_plane, 0)
    partner = trk + 1 - 2 * half
    pl.semaphore_signal(barrier, inc=1, device_id=(partner, me), device_id_type=MESH)
    own.start()
    for load in loads:
        load.start()
    pl.semaphore_wait(barrier, nfrm - 1 + nplane - 1 + 1)

    def vis_copy(k):
        return pltpu.make_async_remote_copy(
            src_ref=vis.at[column(k)],
            dst_ref=vis_recv.at[me],
            send_sem=vis_sem.at[0, k],
            recv_sem=vis_sem.at[1, k],
            device_id=(trk, column(k)),
            device_id_type=MESH,
        )

    def tok_copy(c, k):
        return pltpu.make_async_remote_copy(
            src_ref=tokens.at[column(k), c],
            dst_ref=x_recv.at[me, c],
            send_sem=tok_sem.at[0, c, k],
            recv_sem=tok_sem.at[1, c, k],
            device_id=(trk, column(k)),
            device_id_type=MESH,
        )

    def back_copy(c, k):
        return pltpu.make_async_remote_copy(
            src_ref=stage.at[c, column(k)],
            dst_ref=y_recv.at[me, c],
            send_sem=back_sem.at[0, c, k],
            recv_sem=back_sem.at[1, c, k],
            device_id=(trk, column(k)),
            device_id_type=MESH,
        )

    def each_peer(act):
        def body(k, carry):
            act(k)
            return carry

        lax.fori_loop(1, nfrm, body, 0)

    each_peer(lambda k: vis_copy(k).start())

    def send_chunk(c, carry):
        each_peer(lambda k: tok_copy(c, k).start())
        return carry

    lax.fori_loop(0, chunks, send_chunk, 0)

    for load in loads:
        load.wait()
    cols_to = spread_matrix(False)
    rows_to = spread_matrix(True)

    def pad_cols(n, dst):
        start, cols = offsets[n]
        for b in range(cols // width):
            block = raw[:, start + b * width : start + (b + 1) * width]
            dst[:, b * WIDE : (b + 1) * WIDE] = dot(block, cols_to).astype(bf16)

    def pad_rows(n, dst):
        start, cols = offsets[n]
        dst[...] = dot(rows_to, raw[:, start : start + cols]).astype(bf16)

    pad_cols(0, p_time_qkv)
    pad_rows(1, p_time_o)
    pad_cols(2, p_read_q)
    pad_cols(3, p_read_kv)
    pad_rows(4, p_read_o)
    pad_cols(5, p_write_q)
    pad_cols(6, p_write_kv)
    pad_rows(7, p_write_o)

    virtuals = virt.shape[1]

    def queries(g, carry):
        rows = virt[pl.ds(g * group, group)].reshape(group * virtuals, width).astype(f32)
        normed = (unit(rows) * gains[4:5, :]).astype(bf16)
        vq[pl.ds(g * group, group)] = dot(normed, p_read_q[...]).astype(bf16).reshape(group, virtuals, WIDE)
        return carry

    lax.fori_loop(0, frames // group, queries, 0)

    each_peer(lambda k: vis_copy(k).wait_recv())
    vis_recv[pl.ds(me, 1)] = vis[pl.ds(me, 1)]
    row_bias = jnp.concatenate([vis_recv[s] for s in range(nfrm)], axis=-1)
    time_bias[...] = (row_bias.astype(f32) - 1.0) * PENALTY
    own.wait()
    keys = nfrm * frames

    def attend_chunk(c, carry):
        each_peer(lambda k: tok_copy(c, k).wait_recv())
        rows = jnp.concatenate(
            [x_recv[:, c, t].reshape(keys, width) for t in range(per)], axis=0
        )
        normed = (unit(rows.astype(f32)) * gains[0:1, :]).astype(bf16)
        triple = dot(normed, p_time_qkv[...]).astype(bf16)
        lane = lanes(keys)
        outs = []
        for t in range(per):
            bias = time_bias[pl.ds(c * per + t, 1), :]
            tiles = []
            for p in range(PAIRS):
                q, k, v = (
                    triple[t * keys : (t + 1) * keys, n * WIDE + p * TILE : n * WIDE + (p + 1) * TILE]
                    for n in range(3)
                )
                s = dot_t(q, halves(k, lane)) * SCALE
                parts, dens = [], []
                for h in range(2):
                    sh = s[:, h * keys : (h + 1) * keys] + bias
                    e = jnp.exp(sh - jnp.max(sh, axis=-1, keepdims=True))
                    dens.append(jnp.sum(e, axis=-1, keepdims=True))
                    parts.append(e.astype(bf16))
                num = dot(jnp.concatenate(parts, axis=-1), halves(v, lane))
                tiles.append((num / jnp.where(lane < SLOT, dens[0], dens[1])).astype(bf16))
            outs.append(jnp.concatenate(tiles, axis=-1))
        projected = dot(jnp.concatenate(outs, axis=0), p_time_o[...]).astype(bf16)
        for t in range(per):
            stage[c, :, t] = projected[t * keys : (t + 1) * keys].reshape(nfrm, frames, width)
        each_peer(lambda k: back_copy(c, k).start())
        y_recv[pl.ds(me, 1), pl.ds(c, 1)] = stage[pl.ds(c, 1), pl.ds(me, 1)]
        return carry

    lax.fori_loop(0, chunks, attend_chunk, 0)

    def add_chunk(c, carry):
        each_peer(lambda k: back_copy(c, k).wait_recv())
        for o in range(nfrm):
            total = tok[o, c].astype(f32) + y_recv[o, c].astype(f32)
            total = total.astype(bf16).astype(f32).reshape(per * frames, width)
            start = pl.multiple_of((o * chunks + c) * (per * frames), per * frames)
            for n in range(width // TILE):
                y1t[n, pl.ds(start, per * frames), :] = total[:, n * TILE : (n + 1) * TILE]
        return carry

    lax.fori_loop(0, chunks, add_chunk, 0)
    tracks = y1.shape[1]

    def read_keys(g, carry):
        rows = []
        for n in range(group):
            f = g * group + n
            rows.append(
                jnp.concatenate(
                    [y1t[m, pl.ds(f, tracks, stride=frames), :] for m in range(width // TILE)], axis=-1
                )
            )
        rows = jnp.concatenate(rows, axis=0)
        y1[pl.ds(g * group, group)] = rows.astype(bf16).reshape(group, tracks, width)
        normed = (unit(rows) * gains[1:2, :]).astype(bf16)
        kv2[pl.ds(g * group, group)] = dot(normed, p_read_kv[...]).astype(bf16).reshape(group, tracks, 2 * WIDE)
        return carry

    lax.fori_loop(0, frames // group, read_keys, 0)

    def part_copy(i):
        return pltpu.make_async_remote_copy(
            src_ref=part_send.at[plane(i)],
            dst_ref=part_recv.at[spot],
            send_sem=part_sem.at[0, i],
            recv_sem=part_sem.at[1, i],
            device_id=(plane(i) * 2 + half, me),
            device_id_type=MESH,
        )

    def read_frame(f):
        bias = read_bias[pl.ds(f, 1), :]
        tiles = []
        for p in range(PAIRS):
            at = p * TILE
            num, peak = pair_attention(
                vq[f, :, at : at + TILE], kv2[f, :, at : at + TILE], kv2[f, :, WIDE + at : WIDE + at + TILE], bias
            )
            tiles.append(with_peak(num, peak))
        return jnp.concatenate(tiles, axis=-1)

    def read_step(i, carry):
        part_send[plane(i)] = read_frame(plane(i))
        part_copy(i).start()
        return carry

    lax.fori_loop(1, nplane, read_step, 0)
    part_recv[spot] = read_frame(spot)

    def write_queries(g, carry):
        rows = y1[pl.ds(g * group, group)].reshape(group * tracks, width).astype(f32)
        normed = (unit(rows) * gains[2:3, :]).astype(bf16)
        wq[pl.ds(g * group, group)] = dot(normed, p_write_q[...]).astype(bf16).reshape(group, tracks, WIDE)
        return carry

    lax.fori_loop(0, frames // group, write_queries, 0)

    def each_in_plane(act):
        def body(i, carry):
            act(i)
            return carry

        lax.fori_loop(1, nplane, body, 0)

    each_in_plane(lambda i: part_copy(i).wait_recv())
    for p in range(PAIRS):
        total, peak = merge(part_recv, p)
        cross[pl.ds(half, 1), :, p * TILE : (p + 1) * TILE] = with_peak(total, peak)[None]
    across = pltpu.make_async_remote_copy(
        src_ref=cross.at[half],
        dst_ref=cross.at[half],
        send_sem=cross_sem.at[0],
        recv_sem=cross_sem.at[1],
        device_id=(partner, me),
        device_id_type=MESH,
    )
    across.start()
    across.wait_recv()
    readout = jnp.concatenate([over_den(merge(cross, p)[0]) for p in range(PAIRS)], axis=-1)

    virt1 = (virt[spot].astype(f32) + dot(readout, p_read_o[...])).astype(bf16).astype(f32)
    normed = (unit(virt1) * gains[5:6, :]).astype(bf16)
    middle = gelu(dot(normed, r_vup[...])).astype(bf16)
    vout[spot] = (virt1 + dot(middle, r_vdown[...])).astype(bf16)

    def gather_copy(i):
        return pltpu.make_async_remote_copy(
            src_ref=vout.at[spot],
            dst_ref=vout.at[spot],
            send_sem=gather_sem.at[0, i],
            recv_sem=gather_sem.at[1, i],
            device_id=(plane(i) * 2 + half, me),
            device_id_type=MESH,
        )

    each_in_plane(lambda i: gather_copy(i).start())

    def write_group(g, carry):
        for n in range(group):
            i = g * group + n

            @pl.when(i > 0)
            def _():
                gather_copy(i).wait_recv()

        where = [lax.rem(spot - (g * group + n) + nplane, nplane) for n in range(group)]
        rows = jnp.concatenate([vout[f] for f in where], axis=0).astype(f32)
        normed = (unit(rows) * gains[6:7, :]).astype(bf16)
        pairs = dot(normed, p_write_kv[...]).astype(bf16)
        outs = []
        for n, f in enumerate(where):
            tiles = []
            for p in range(PAIRS):
                at = p * TILE
                block = pairs[n * virtuals : (n + 1) * virtuals]
                num, _ = pair_attention(
                    wq[f, :, at : at + TILE], block[:, at : at + TILE], block[:, WIDE + at : WIDE + at + TILE], None
                )
                tiles.append(over_den(num))
            outs.append(jnp.concatenate(tiles, axis=-1))
        first = jnp.concatenate([y1[f] for f in where], axis=0).astype(f32)
        second = first + dot(jnp.concatenate(outs, axis=0), p_write_o[...])
        second = second.astype(bf16).astype(f32)
        normed = (unit(second) * gains[3:4, :]).astype(bf16)
        middle = gelu(dot(normed, r_up[...])).astype(bf16)
        final = second + dot(middle, r_down[...])
        for n, f in enumerate(where):
            for m in range(width // TILE):
                outt[m, pl.ds(f, tracks, stride=frames), :] = final[
                    n * tracks : (n + 1) * tracks, m * TILE : (m + 1) * TILE
                ]
        return carry

    lax.fori_loop(0, frames // group, write_group, 0)
    virt_done = pltpu.make_async_copy(vout, virt_out, out_sem)
    virt_done.start()
    block = tracks // 8

    def finish(b, carry):
        rows = pl.multiple_of(b * (block * frames), block * frames)
        for m in range(width // TILE):
            part = outt[m, pl.ds(rows, block * frames), :].astype(bf16)
            track_out[pl.ds(b * block, block), :, m * TILE : (m + 1) * TILE] = part.reshape(block, frames, TILE)
        return carry

    lax.fori_loop(0, 8, finish, 0)

    each_peer(lambda k: vis_copy(k).wait_send())

    def drain(c, carry):
        each_peer(lambda k: tok_copy(c, k).wait_send())
        each_peer(lambda k: back_copy(c, k).wait_send())
        return carry

    lax.fori_loop(0, chunks, drain, 0)
    each_in_plane(lambda i: part_copy(i).wait_send())
    across.wait_send()
    each_in_plane(lambda i: gather_copy(i).wait_send())
    virt_done.wait()


def shards(tokens, visible, virtual, gains, *weights):
    tracks, frames, width = tokens.shape
    nfrm, nplane = lax.axis_size("frm"), lax.axis_size("trk") // 2
    virtuals = virtual.shape[1]
    owned = tracks // nfrm
    chunks = 4
    per = owned // chunks
    hidden = weights[8].shape[1]
    dims = (nfrm, nplane, chunks, per, frames)
    cut = tokens.reshape(nfrm, chunks, per, frames, width)
    bias = ((visible.astype(f32) - 1.0) * PENALTY).T
    bias = jnp.concatenate([bias, bias], axis=1)
    narrow = (nfrm, chunks, per, frames, width)
    vmem, anywhere = pl.BlockSpec(memory_space=pltpu.VMEM), pl.BlockSpec(memory_space=pl.ANY)
    dma = pltpu.SemaphoreType.DMA
    raw_cols = sum(w.shape[1] for w in weights[:8])
    out = pl.pallas_call(
        functools.partial(kernel, dims),
        out_shape=(
            jax.ShapeDtypeStruct((tracks, frames, width), bf16),
            jax.ShapeDtypeStruct((frames, virtuals, width), bf16),
        ),
        in_specs=[anywhere, vmem, vmem, anywhere, vmem] + [anywhere] * 12,
        out_specs=(vmem, anywhere),
        scratch_shapes=[
            pltpu.VMEM(narrow, bf16),
            pltpu.VMEM(narrow, bf16),
            pltpu.VMEM((chunks, nfrm, per, frames, width), bf16),
            pltpu.VMEM(narrow, bf16),
            pltpu.VMEM((nfrm, owned, frames), jnp.int32),
            pltpu.VMEM((owned, nfrm * frames), f32),
            pltpu.VMEM((width // TILE, tracks * frames, TILE), f32),
            pltpu.VMEM((frames, tracks, width), bf16),
            pltpu.VMEM((frames, virtuals, width), bf16),
            pltpu.VMEM((frames, virtuals, WIDE), bf16),
            pltpu.VMEM((frames, tracks, 2 * WIDE), bf16),
            pltpu.VMEM((frames, tracks, WIDE), bf16),
            pltpu.VMEM((nplane, virtuals, WIDE), bf16),
            pltpu.VMEM((nplane, virtuals, WIDE), bf16),
            pltpu.VMEM((2, virtuals, WIDE), bf16),
            pltpu.VMEM((frames, virtuals, width), bf16),
            pltpu.VMEM((width // TILE, tracks * frames, TILE), f32),
            pltpu.VMEM((width, raw_cols), bf16),
            pltpu.VMEM((width, hidden), bf16),
            pltpu.VMEM((hidden, width), bf16),
            pltpu.VMEM((width, hidden), bf16),
            pltpu.VMEM((hidden, width), bf16),
            pltpu.VMEM((width, 3 * WIDE), bf16),
            pltpu.VMEM((WIDE, width), bf16),
            pltpu.VMEM((width, WIDE), bf16),
            pltpu.VMEM((width, 2 * WIDE), bf16),
            pltpu.VMEM((WIDE, width), bf16),
            pltpu.VMEM((width, WIDE), bf16),
            pltpu.VMEM((width, 2 * WIDE), bf16),
            pltpu.VMEM((WIDE, width), bf16),
            dma((14,)),
            dma,
            dma((2, nfrm)),
            dma((2, chunks, nfrm)),
            dma((2, chunks, nfrm)),
            dma((2, nplane)),
            dma((2,)),
            dma((2, nplane)),
            dma,
        ],
        compiler_params=pltpu.CompilerParams(
            collective_id=0, has_side_effects=True, vmem_limit_bytes=56 * 1024 * 1024
        ),
    )(cut, visible.reshape(nfrm, owned, frames), bias, virtual, gains, *weights)
    return out


def solution(mesh):
    in_specs = (P("trk", "frm", None), P("trk", "frm"), P("frm", None, None)) + (P(),) * 13
    out_specs = (P("trk", "frm", None), P("frm", None, None))
    return jax.shard_map(shards, mesh=mesh, in_specs=in_specs, out_specs=out_specs, check_vma=False)
```

```python
import functools
import math

import jax
import jax.numpy as jnp
from jax import lax
from jax.experimental import pallas as pl
from jax.experimental.pallas import tpu as pltpu
from jax.sharding import PartitionSpec as P

HEADS = 8
HEAD = 48
SLOT = 64
TILE = 128
PAIRS = HEADS // 2
WIDE = HEADS * SLOT
PENALTY = 4.0
EPSILON = 1e-05
SCALE = 1.0 / math.sqrt(HEAD)
MESH = pl.DeviceIdType.MESH
f32 = jnp.float32
bf16 = jnp.bfloat16


def dot(a, b):
    return lax.dot_general(a, b, (((1,), (0,)), ((), ())), preferred_element_type=f32)


def dot_t(a, b):
    return lax.dot_general(a, b, (((1,), (1,)), ((), ())), preferred_element_type=f32)


def unit(x):
    center = x - jnp.mean(x, axis=-1, keepdims=True)
    spread = jnp.mean(center * center, axis=-1, keepdims=True)
    return center * lax.rsqrt(spread + EPSILON)


def gelu(x):
    return jax.nn.gelu(x, approximate=True)


def spread_matrix(rows_are_padded):
    shape = (WIDE, HEADS * HEAD) if rows_are_padded else (HEADS * HEAD, WIDE)
    tight = lax.broadcasted_iota(jnp.int32, shape, 1 if rows_are_padded else 0)
    padded = lax.broadcasted_iota(jnp.int32, shape, 0 if rows_are_padded else 1)
    target = tight
    for h in range(1, HEADS):
        target = target + jnp.where(tight >= HEAD * h, SLOT - HEAD, 0)
    return jnp.where(target == padded, 1.0, 0.0).astype(bf16)


def halves(x, lane):
    zero = jnp.zeros_like(x)
    return jnp.concatenate(
        [jnp.where(lane < SLOT, x, zero), jnp.where(lane < SLOT, zero, x)], axis=0
    )


def lanes(rows):
    return lax.broadcasted_iota(jnp.int32, (rows, TILE), 1)


def slot_lanes(rows):
    lane = lanes(rows)
    return jnp.where(lane < SLOT, lane, lane - SLOT)


def pair_attention(qs, ks, vs, biases):
    lane_k, lane_q = lanes(ks[0].shape[0]), lanes(qs[0].shape[0])
    marked = slot_lanes(ks[0].shape[0]) == HEAD
    vs = [jnp.where(marked, jnp.ones_like(v), v) for v in vs]
    scores = [dot_t(q, halves(k, lane_k)) * SCALE for q, k in zip(qs, ks)]
    if biases is not None:
        scores = [s + b for s, b in zip(scores, biases)]
    left = lane_q < SLOT
    first = [jnp.max(jnp.where(left, s, -jnp.inf), axis=-1, keepdims=True) for s in scores]
    second = [jnp.max(jnp.where(left, -jnp.inf, s), axis=-1, keepdims=True) for s in scores]
    peaks = [jnp.where(left, x, y) for x, y in zip(first, second)]
    expos = [jnp.exp(s - p).astype(bf16) for s, p in zip(scores, peaks)]
    return [dot(e, halves(v, lane_k)) for e, v in zip(expos, vs)], peaks


def with_peak(num, peak):
    place = slot_lanes(num.shape[0])
    high = peak.astype(bf16).astype(f32)
    rest = peak - high
    mid = rest.astype(bf16).astype(f32)
    low = rest - mid
    num = jnp.where(place == HEAD + 1, high, num)
    num = jnp.where(place == HEAD + 2, mid, num)
    num = jnp.where(place == HEAD + 3, low, num)
    return num.astype(bf16)


def over_den(num):
    rows = num.shape[0]
    den = jnp.where(lanes(rows) < SLOT, num[:, HEAD : HEAD + 1], num[:, SLOT + HEAD : SLOT + HEAD + 1])
    return jnp.where(slot_lanes(rows) < HEAD, num / den, 0.0).astype(bf16)


def merge(part):
    count, rows = part.shape[0], part.shape[1]
    row = lax.broadcasted_iota(jnp.int32, (TILE, TILE), 0)
    col = lax.broadcasted_iota(jnp.int32, (TILE, TILE), 1)
    same = (row < SLOT) == (col < SLOT)
    place = jnp.where(row < SLOT, row, row - SLOT)
    pick = same & (place > HEAD) & (place < HEAD + 4)
    peaks = dot(part.reshape(count * rows, TILE), jnp.where(pick, 1.0, 0.0).astype(bf16))
    peaks = peaks.reshape(count, rows, TILE)
    peak = jnp.max(peaks, axis=0)
    total = jnp.sum(jnp.exp(peaks - peak[None]) * part.astype(f32), axis=0)
    return total, peak


def merge_tiles(value):
    return jnp.concatenate(
        [
            with_peak(*merge(value[:, :, at : at + TILE]))
            for at in range(0, value.shape[-1], TILE)
        ],
        axis=-1,
    )


def kernel(
    dims,
    tokens,
    vis,
    virtual,
    gains,
    w_time_qkv,
    w_time_o,
    w_read_q,
    w_read_kv,
    w_read_o,
    w_write_q,
    w_write_kv,
    w_write_o,
    w_up,
    w_down,
    v_up,
    v_down,
    track_out,
    virt_out,
    tok,
    x_recv,
    qkv,
    stage,
    y_recv,
    vis_recv,
    time_bias,
    read_bias,
    y1t,
    y1,
    virt,
    vq,
    kv2,
    wq,
    pay,
    one_x,
    one_y,
    mid_x,
    mid_y,
    two_x,
    two_y,
    cross,
    vout,
    outv,
    raw,
    r_up,
    r_down,
    r_vup,
    r_vdown,
    p_time_qkv,
    p_time_o,
    p_read_q,
    p_read_kv,
    p_read_o,
    p_write_q,
    p_write_kv,
    p_write_o,
    load_sem,
    own_sem,
    vis_sem,
    tok_sem,
    back_sem,
    part_sem,
    cross_sem,
    gather_sem,
    out_sem,
):
    nfrm, px, py, chunks, per, frames, parts = dims
    nplane = px * py
    trk, me = lax.axis_index("trk"), lax.axis_index("frm")
    spot, half = lax.div(trk, 2), lax.rem(trk, 2)
    x, y = lax.div(spot, py), lax.rem(spot, py)
    width = HEADS * HEAD
    few = frames // parts
    owned = chunks * per
    keys = nfrm * frames
    tracks, virtuals = y1.shape[1], vq.shape[1]
    unit_rows = few * virtuals // nplane
    batch = owned // 2
    group = min(4, few)

    def column(k):
        return lax.rem(me + k, nfrm)

    def along_x(i):
        return lax.rem(x + i, px)

    def along_y(i):
        return lax.rem(y + i, py)

    def place(xx, yy):
        return ((xx * py + yy) * 2 + half, me)

    def in_plane(i):
        other = lax.rem(spot + i, nplane)
        return (other * 2 + half, me)

    def remote(src, dst, sems, where):
        return pltpu.make_async_remote_copy(
            src_ref=src,
            dst_ref=dst,
            send_sem=sems[0],
            recv_sem=sems[1],
            device_id=where,
            device_id_type=MESH,
        )

    def each(count, act):
        def body(k, carry):
            act(k)
            return carry

        lax.fori_loop(1, count, body, 0)

    weights = (w_time_qkv, w_time_o, w_read_q, w_read_kv, w_read_o, w_write_q, w_write_kv, w_write_o)
    offsets = []
    at = 0
    loads = []
    for n, w in enumerate(weights):
        cols = w.shape[1]
        offsets.append((at, cols))
        loads.append(pltpu.make_async_copy(w, raw.at[:, pl.ds(at, cols)], load_sem.at[n]))
        at += cols
    for w, dst in ((w_up, r_up), (w_down, r_down), (v_up, r_vup), (v_down, r_vdown), (virtual, virt), (tokens, tok)):
        loads.append(pltpu.make_async_copy(w, dst, load_sem.at[len(loads)]))
    own = pltpu.make_async_copy(tokens.at[me], x_recv.at[me], own_sem)

    barrier = pltpu.get_barrier_semaphore()
    partner = (trk + 1 - 2 * half, me)
    pl.semaphore_signal(barrier, inc=1, device_id=partner, device_id_type=MESH)
    each(
        nfrm,
        lambda k: pl.semaphore_signal(barrier, inc=1, device_id=(trk, column(k)), device_id_type=MESH),
    )
    each(
        nplane,
        lambda i: pl.semaphore_signal(barrier, inc=1, device_id=in_plane(i), device_id_type=MESH),
    )
    pl.semaphore_wait(barrier, nfrm - 1 + nplane - 1 + 1)

    def vis_rows(p):
        return pl.ds(pl.multiple_of(p * owned, owned), owned)

    def vis_copy(k):
        return remote(
            vis.at[vis_rows(column(k))],
            vis_recv.at[me],
            (vis_sem.at[0, k], vis_sem.at[1, k]),
            (trk, column(k)),
        )

    def tok_copy(c, k):
        return remote(
            tokens.at[column(k), pl.ds(c * per, per)],
            x_recv.at[me, pl.ds(c * per, per)],
            (tok_sem.at[0, c, k], tok_sem.at[1, c, k]),
            (trk, column(k)),
        )

    def back_copy(n, k):
        return remote(
            stage.at[n, column(k)],
            y_recv.at[n, me],
            (back_sem.at[0, n, k], back_sem.at[1, n, k]),
            (trk, column(k)),
        )

    each(nfrm, lambda k: vis_copy(k).start())
    for c in range(chunks):
        each(nfrm, lambda k: tok_copy(c, k).start())
    own.start()
    for load in loads:
        load.start()

    for load in loads:
        load.wait()
    cols_to = spread_matrix(False)
    rows_to = spread_matrix(True)

    def pad_cols(n, dst):
        start, cols = offsets[n]
        for b in range(cols // width):
            block = raw[:, start + b * width : start + (b + 1) * width]
            dst[:, b * WIDE : (b + 1) * WIDE] = dot(block, cols_to).astype(bf16)

    def pad_rows(n, dst):
        start, cols = offsets[n]
        dst[...] = dot(rows_to, raw[:, start : start + cols]).astype(bf16)

    pad_cols(0, p_time_qkv)
    pad_rows(1, p_time_o)
    pad_cols(2, p_read_q)
    pad_cols(3, p_read_kv)
    pad_rows(4, p_read_o)
    pad_cols(5, p_write_q)
    pad_cols(6, p_write_kv)
    pad_rows(7, p_write_o)

    for h in range(parts):
        rows = virt[h].reshape(few * virtuals, width).astype(f32)
        normed = (unit(rows) * gains[4:5, :]).astype(bf16)
        queries = dot(normed, p_read_q[...]).astype(bf16)
        vq[h * few : (h + 1) * few] = queries.reshape(few, virtuals, WIDE)

    flipped = jnp.transpose((vis[...].astype(f32) - 1.0) * PENALTY)
    read_bias[...] = jnp.concatenate([flipped, flipped], axis=-1)

    each(nfrm, lambda k: vis_copy(k).wait_recv())
    vis_recv[pl.ds(me, 1)] = vis[vis_rows(me)][None]
    row_bias = jnp.concatenate(
        [vis_recv[s][:, h * few : (h + 1) * few] for h in range(parts) for s in range(nfrm)], axis=-1
    )
    time_bias[...] = (row_bias.astype(f32) - 1.0) * PENALTY
    own.wait()

    def project(c, carry):
        each(nfrm, lambda k: tok_copy(c, k).wait_recv())
        rows = []
        for t in range(per):
            blocks = [x_recv[s, c * per + t].astype(f32) for s in range(nfrm)]
            rows += [b[h * few : (h + 1) * few] for h in range(parts) for b in blocks]
        rows = jnp.concatenate(rows, axis=0)
        normed = (unit(rows) * gains[0:1, :]).astype(bf16)
        triple = dot(normed, p_time_qkv[...]).astype(bf16)
        qkv[pl.ds(c * per, per)] = triple.reshape(per, keys, 3 * WIDE)
        return carry

    lax.fori_loop(0, chunks, project, 0)
    asked = keys // parts

    def attend(n, carry):
        h, first = lax.div(n, 2), lax.rem(n, 2) * batch
        lane_k, lane_q = lanes(keys), lanes(asked)
        blocks = [(t, p) for t in range(batch) for p in range(PAIRS)]
        bias = [time_bias[pl.ds(first + t, 1), :] for t in range(batch)]
        bias = [jnp.concatenate([b, b], axis=-1) for b in bias]

        def piece(m, t, p):
            cols = slice(m * WIDE + p * TILE, m * WIDE + (p + 1) * TILE)
            if m == 0:
                return qkv[first + t, pl.ds(pl.multiple_of(h * asked, asked), asked), cols]
            return qkv[first + t, :, cols]

        scores = [dot_t(piece(0, t, p), halves(piece(1, t, p), lane_k)) * SCALE + bias[t] for t, p in blocks]
        heads = [s[:, m * keys : (m + 1) * keys] for s in scores for m in range(2)]
        peaks = [jnp.max(s, axis=-1, keepdims=True) for s in heads]
        expos = [jnp.exp(s - m) for s, m in zip(heads, peaks)]
        dens = [jnp.sum(e, axis=-1, keepdims=True) for e in expos]
        expos = [e.astype(bf16) for e in expos]
        nums = [
            dot(jnp.concatenate(expos[2 * m : 2 * m + 2], axis=-1), halves(piece(2, t, p), lane_k))
            for m, (t, p) in enumerate(blocks)
        ]
        tiles = [
            (num / jnp.where(lane_q < SLOT, dens[2 * m], dens[2 * m + 1])).astype(bf16)
            for m, num in enumerate(nums)
        ]
        outs = [jnp.concatenate(tiles[t * PAIRS : (t + 1) * PAIRS], axis=-1) for t in range(batch)]
        projected = dot(jnp.concatenate(outs, axis=0), p_time_o[...])
        for s in range(nfrm):
            mine = [
                projected[t * asked + s * few : t * asked + (s + 1) * few] for t in range(batch)
            ]
            stage[n, s] = jnp.concatenate(mine, axis=0).astype(bf16)
        each(nfrm, lambda k: back_copy(n, k).start())
        y_recv[pl.ds(n, 1), pl.ds(me, 1)] = stage[pl.ds(n, 1), pl.ds(me, 1)]
        return carry

    lax.fori_loop(0, 2 * parts, attend, 0)

    def add(h):
        for b in range(2):
            n = h * 2 + b
            each(nfrm, lambda k: back_copy(n, k).wait_recv())
            for o in range(nfrm):
                old = tok[o, b * batch : (b + 1) * batch].astype(f32)[:, h * few : (h + 1) * few]
                total = old + y_recv[n, o].astype(f32).reshape(batch, few, width)
                total = total.astype(bf16).astype(f32).reshape(batch * few, width)
                start = (o * owned + b * batch) * few
                for m in range(width // TILE):
                    y1t[m, start : start + batch * few, :] = total[:, m * TILE : (m + 1) * TILE]
        rows = []
        for f in range(few):
            rows.append(
                jnp.concatenate(
                    [y1t[m, pl.ds(f, tracks, stride=few), :] for m in range(width // TILE)], axis=-1
                )
            )
        rows = jnp.concatenate(rows, axis=0)
        span = slice(h * few, (h + 1) * few)
        y1[span] = rows.astype(bf16).reshape(few, tracks, width)
        normed = (unit(rows) * gains[1:2, :]).astype(bf16)
        kv2[span] = dot(normed, p_read_kv[...]).astype(bf16).reshape(few, tracks, 2 * WIDE)

    def write_queries(h):
        span = slice(h * few, (h + 1) * few)
        rows = y1[span].reshape(few * tracks, width).astype(f32)
        normed = (unit(rows) * gains[2:3, :]).astype(bf16)
        wq[span] = dot(normed, p_write_q[...]).astype(bf16).reshape(few, tracks, WIDE)

    low, high = pl.ds(0, WIDE // 2), pl.ds(WIDE // 2, WIDE // 2)

    def one_x_copy(h, i):
        return remote(
            pay.at[h, along_x(i), :, :, low],
            one_x.at[h, x],
            (part_sem.at[0, h, 0, i], part_sem.at[1, h, 0, i]),
            place(along_x(i), y),
        )

    def one_y_copy(h, i):
        return remote(
            pay.at[h, :, along_y(i), :, high],
            one_y.at[h, y],
            (part_sem.at[0, h, 1, i], part_sem.at[1, h, 1, i]),
            place(x, along_y(i)),
        )

    def two_y_copy(h, i):
        return remote(
            mid_x.at[h, along_y(i)],
            two_y.at[h, y],
            (part_sem.at[0, h, 2, i], part_sem.at[1, h, 2, i]),
            place(x, along_y(i)),
        )

    def two_x_copy(h, i):
        return remote(
            mid_y.at[h, along_x(i)],
            two_x.at[h, x],
            (part_sem.at[0, h, 3, i], part_sem.at[1, h, 3, i]),
            place(along_x(i), y),
        )

    def across(h):
        return remote(
            cross.at[h, half], cross.at[h, half], (cross_sem.at[0, h], cross_sem.at[1, h]), partner
        )

    def gather_copy(h, i):
        return remote(
            vout.at[h, x, y],
            vout.at[h, x, y],
            (gather_sem.at[0, h, i], gather_sem.at[1, h, i]),
            in_plane(i),
        )

    def read(h):
        at = [p * TILE for p in range(PAIRS)]
        for g in range(few // group):
            inside = [h * few + g * group + n for n in range(group)]
            nums, peaks = pair_attention(
                [vq[f, :, a : a + TILE] for f in inside for a in at],
                [kv2[f, :, a : a + TILE] for f in inside for a in at],
                [kv2[f, :, WIDE + a : WIDE + a + TILE] for f in inside for a in at],
                [read_bias[f : f + 1, :] for f in inside for a in at],
            )
            tiles = [with_peak(num, peak) for num, peak in zip(nums, peaks)]
            for n in range(group):
                rows = jnp.concatenate(tiles[n * PAIRS : (n + 1) * PAIRS], axis=-1)
                for r in range(0, virtuals, unit_rows):
                    u = ((g * group + n) * virtuals + r) // unit_rows
                    pay[h, u // py, u % py] = rows[r : r + unit_rows]
        each(px, lambda i: one_x_copy(h, i).start())
        each(py, lambda i: one_y_copy(h, i).start())
        one_x[pl.ds(h, 1), pl.ds(x, 1)] = pay[pl.ds(h, 1), pl.ds(x, 1), :, :, : WIDE // 2]
        one_y[h, pl.ds(y, 1)] = pay[h, :, pl.ds(y, 1), :, WIDE // 2 :].reshape(1, px, unit_rows, WIDE // 2)

    def middle_step(h):
        each(px, lambda i: one_x_copy(h, i).wait_recv())
        merged = merge_tiles(one_x[h].reshape(px, py * unit_rows, WIDE // 2))
        mid_x[h] = merged.reshape(py, unit_rows, WIDE // 2)
        each(py, lambda i: two_y_copy(h, i).start())
        two_y[h, pl.ds(y, 1)] = mid_x[h, pl.ds(y, 1)]
        each(py, lambda i: one_y_copy(h, i).wait_recv())
        merged = merge_tiles(one_y[h].reshape(py, px * unit_rows, WIDE // 2))
        mid_y[h] = merged.reshape(px, unit_rows, WIDE // 2)
        each(px, lambda i: two_x_copy(h, i).start())
        two_x[h, pl.ds(x, 1)] = mid_y[h, pl.ds(x, 1)]

    def cross_step(h):
        each(py, lambda i: two_y_copy(h, i).wait_recv())
        lower = merge_tiles(two_y[h])
        each(px, lambda i: two_x_copy(h, i).wait_recv())
        upper = merge_tiles(two_x[h])
        cross[h, pl.ds(half, 1)] = jnp.concatenate([lower, upper], axis=-1)[None]
        across(h).start()

    def virtual_step(h):
        across(h).wait_recv()
        both = cross[h]
        readout = jnp.concatenate(
            [over_den(merge(both[:, :, p * TILE : (p + 1) * TILE])[0]) for p in range(PAIRS)], axis=-1
        )
        virt1 = (virt[h, x, y].astype(f32) + dot(readout, p_read_o[...])).astype(bf16).astype(f32)
        normed = (unit(virt1) * gains[5:6, :]).astype(bf16)
        middle = gelu(dot(normed, r_vup[...])).astype(bf16)
        vout[h, x, y] = (virt1 + dot(middle, r_vdown[...])).astype(bf16)
        each(nplane, lambda i: gather_copy(h, i).start())

    def out_copy(h, g):
        span = pl.ds(h * few + g * group, group)
        return pltpu.make_async_copy(outv.at[span], track_out.at[span], out_sem.at[h * (few // group) + g])

    def write(h, g):
        if g == 0:
            each(nplane, lambda i: gather_copy(h, i).wait_recv())
        count = group * virtuals // unit_rows
        units = [g * count + n for n in range(count)]
        rows = jnp.concatenate([vout[h, u // py, u % py] for u in units], axis=0).astype(f32)
        normed = (unit(rows) * gains[6:7, :]).astype(bf16)
        pairs = dot(normed, p_write_kv[...]).astype(bf16)
        span = slice(h * few + g * group, h * few + (g + 1) * group)
        at = [p * TILE for p in range(PAIRS)]
        blocks = [pairs[n * virtuals : (n + 1) * virtuals] for n in range(group)]
        nums, _ = pair_attention(
            [wq[f, :, a : a + TILE] for f in range(span.start, span.stop) for a in at],
            [block[:, a : a + TILE] for block in blocks for a in at],
            [block[:, WIDE + a : WIDE + a + TILE] for block in blocks for a in at],
            None,
        )
        tiles = [over_den(num) for num in nums]
        outs = [jnp.concatenate(tiles[n * PAIRS : (n + 1) * PAIRS], axis=-1) for n in range(group)]
        first = y1[span].reshape(group * tracks, width).astype(f32)
        second = first + dot(jnp.concatenate(outs, axis=0), p_write_o[...])
        second = second.astype(bf16).astype(f32)
        normed = (unit(second) * gains[3:4, :]).astype(bf16)
        middle = gelu(dot(normed, r_up[...])).astype(bf16)
        final = second + dot(middle, r_down[...])
        outv[span] = final.astype(bf16).reshape(group, tracks, width)
        out_copy(h, g).start()

    add(0)
    read(0)
    write_queries(0)
    middle_step(0)
    cross_step(0)
    add(1)
    read(1)
    virtual_step(0)
    write_queries(1)
    middle_step(1)
    cross_step(1)
    write(0, 0)
    virtual_step(1)
    for g in range(1, few // group):
        write(0, g)
    for g in range(few // group):
        write(1, g)

    virt_done = pltpu.make_async_copy(vout, virt_out, own_sem)
    virt_done.start()

    each(nfrm, lambda k: vis_copy(k).wait_send())
    for c in range(chunks):
        each(nfrm, lambda k: tok_copy(c, k).wait_send())
    for n in range(2 * parts):
        each(nfrm, lambda k: back_copy(n, k).wait_send())
    for h in range(parts):
        each(px, lambda i: one_x_copy(h, i).wait_send())
        each(py, lambda i: one_y_copy(h, i).wait_send())
        each(py, lambda i: two_y_copy(h, i).wait_send())
        each(px, lambda i: two_x_copy(h, i).wait_send())
        across(h).wait_send()
        each(nplane, lambda i: gather_copy(h, i).wait_send())
        for g in range(few // group):
            out_copy(h, g).wait()
    virt_done.wait()


def shards(tokens, visible, virtual, gains, *weights):
    tracks, frames, width = tokens.shape
    nfrm, nplane = lax.axis_size("frm"), lax.axis_size("trk") // 2
    virtuals = virtual.shape[1]
    py = math.isqrt(nplane)
    px = nplane // py
    owned = tracks // nfrm
    chunks, parts = 4, 2
    per = owned // chunks
    few = frames // parts
    unit_rows = few * virtuals // nplane
    hidden = weights[8].shape[1]
    keys = nfrm * frames
    dims = (nfrm, px, py, chunks, per, frames, parts)
    narrow = (nfrm, owned, frames, width)
    shares = (parts, px, py, unit_rows, width)
    vmem, anywhere = pl.BlockSpec(memory_space=pltpu.VMEM), pl.BlockSpec(memory_space=pl.ANY)
    dma = pltpu.SemaphoreType.DMA
    raw_cols = sum(w.shape[1] for w in weights[:8])
    track_out, virt_out = pl.pallas_call(
        functools.partial(kernel, dims),
        out_shape=(
            jax.ShapeDtypeStruct((frames, tracks, width), bf16),
            jax.ShapeDtypeStruct(shares, bf16),
        ),
        in_specs=[anywhere, vmem, anywhere, vmem] + [anywhere] * 12,
        out_specs=(anywhere, anywhere),
        scratch_shapes=[
            pltpu.VMEM(narrow, bf16),
            pltpu.VMEM(narrow, bf16),
            pltpu.VMEM((owned, keys, 3 * WIDE), bf16),
            pltpu.VMEM((2 * parts, nfrm, owned // 2 * few, width), bf16),
            pltpu.VMEM((2 * parts, nfrm, owned // 2 * few, width), bf16),
            pltpu.VMEM((nfrm, owned, frames), jnp.int32),
            pltpu.VMEM((owned, keys), f32),
            pltpu.VMEM((frames, 2 * tracks), f32),
            pltpu.VMEM((width // TILE, tracks * few, TILE), f32),
            pltpu.VMEM((frames, tracks, width), bf16),
            pltpu.VMEM(shares, bf16),
            pltpu.VMEM((frames, virtuals, WIDE), bf16),
            pltpu.VMEM((frames, tracks, 2 * WIDE), bf16),
            pltpu.VMEM((frames, tracks, WIDE), bf16),
            pltpu.VMEM((parts, px, py, unit_rows, WIDE), bf16),
            pltpu.VMEM((parts, px, py, unit_rows, WIDE // 2), bf16),
            pltpu.VMEM((parts, py, px, unit_rows, WIDE // 2), bf16),
            pltpu.VMEM((parts, py, unit_rows, WIDE // 2), bf16),
            pltpu.VMEM((parts, px, unit_rows, WIDE // 2), bf16),
            pltpu.VMEM((parts, px, unit_rows, WIDE // 2), bf16),
            pltpu.VMEM((parts, py, unit_rows, WIDE // 2), bf16),
            pltpu.VMEM((parts, 2, unit_rows, WIDE), bf16),
            pltpu.VMEM(shares, bf16),
            pltpu.VMEM((frames, tracks, width), bf16),
            pltpu.VMEM((width, raw_cols), bf16),
            pltpu.VMEM((width, hidden), bf16),
            pltpu.VMEM((hidden, width), bf16),
            pltpu.VMEM((width, hidden), bf16),
            pltpu.VMEM((hidden, width), bf16),
            pltpu.VMEM((width, 3 * WIDE), bf16),
            pltpu.VMEM((WIDE, width), bf16),
            pltpu.VMEM((width, WIDE), bf16),
            pltpu.VMEM((width, 2 * WIDE), bf16),
            pltpu.VMEM((WIDE, width), bf16),
            pltpu.VMEM((width, WIDE), bf16),
            pltpu.VMEM((width, 2 * WIDE), bf16),
            pltpu.VMEM((WIDE, width), bf16),
            dma((14,)),
            dma,
            dma((2, nfrm)),
            dma((2, chunks, nfrm)),
            dma((2, 2 * parts, nfrm)),
            dma((2, parts, 4, max(px, py))),
            dma((2, parts)),
            dma((2, parts, nplane)),
            dma((frames,)),
        ],
        compiler_params=pltpu.CompilerParams(
            collective_id=0, has_side_effects=True, vmem_limit_bytes=56 * 1024 * 1024
        ),
    )(tokens.reshape(narrow), visible, virtual.reshape(shares), gains, *weights)
    return jnp.transpose(track_out, (1, 0, 2)), virt_out.reshape(frames, virtuals, width)


def solution(mesh):
    in_specs = (P("trk", "frm", None), P("trk", "frm"), P("frm", None, None)) + (P(),) * 13
    out_specs = (P("trk", "frm", None), P("frm", None, None))
    return jax.shard_map(shards, mesh=mesh, in_specs=in_specs, out_specs=out_specs, check_vma=False)
```

```python
import functools
import math

import jax
import jax.numpy as jnp
from jax import lax
from jax.experimental import pallas as pl
from jax.experimental.pallas import tpu as pltpu
from jax.sharding import PartitionSpec as P

HEADS = 8
HEAD = 48
SLOT = 64
TILE = 128
PAIRS = HEADS // 2
WIDE = HEADS * SLOT
PENALTY = 4.0
EPSILON = 1e-05
SCALE = 1.0 / math.sqrt(HEAD)
MESH = pl.DeviceIdType.MESH
f32 = jnp.float32
bf16 = jnp.bfloat16


def dot(a, b):
    return lax.dot_general(a, b, (((1,), (0,)), ((), ())), preferred_element_type=f32)


def dot_t(a, b):
    return lax.dot_general(a, b, (((1,), (1,)), ((), ())), preferred_element_type=f32)


def unit(x):
    center = x - jnp.mean(x, axis=-1, keepdims=True)
    spread = jnp.mean(center * center, axis=-1, keepdims=True)
    return center * lax.rsqrt(spread + EPSILON)


def gelu(x):
    return jax.nn.gelu(x, approximate=True)


def spread_matrix(rows_are_padded):
    shape = (WIDE, HEADS * HEAD) if rows_are_padded else (HEADS * HEAD, WIDE)
    tight = lax.broadcasted_iota(jnp.int32, shape, 1 if rows_are_padded else 0)
    padded = lax.broadcasted_iota(jnp.int32, shape, 0 if rows_are_padded else 1)
    target = tight
    for h in range(1, HEADS):
        target = target + jnp.where(tight >= HEAD * h, SLOT - HEAD, 0)
    return jnp.where(target == padded, 1.0, 0.0).astype(bf16)


def halves(x, lane):
    zero = jnp.zeros_like(x)
    return jnp.concatenate(
        [jnp.where(lane < SLOT, x, zero), jnp.where(lane < SLOT, zero, x)], axis=0
    )


def lanes(rows):
    return lax.broadcasted_iota(jnp.int32, (rows, TILE), 1)


def slot_lanes(rows):
    lane = lanes(rows)
    return jnp.where(lane < SLOT, lane, lane - SLOT)


def sum_columns(keys):
    row = lax.broadcasted_iota(jnp.int32, (2 * keys, TILE), 0)
    col = lax.broadcasted_iota(jnp.int32, (2 * keys, TILE), 1)
    return jnp.where((row < keys) == (col < SLOT), 1.0, 0.0).astype(bf16)


def pair_attention(qs, ks, vs, biases):
    keys = ks[0].shape[0]
    lane_k, lane_q = lanes(keys), lanes(qs[0].shape[0])
    ones = sum_columns(keys)
    scores = [dot_t(q, halves(k, lane_k)) * SCALE for q, k in zip(qs, ks)]
    if biases is not None:
        scores = [s + b for s, b in zip(scores, biases)]
    left = lane_q < SLOT
    first = [jnp.max(jnp.where(left, s, -jnp.inf), axis=-1, keepdims=True) for s in scores]
    second = [jnp.max(jnp.where(left, -jnp.inf, s), axis=-1, keepdims=True) for s in scores]
    peaks = [jnp.where(left, x, y) for x, y in zip(first, second)]
    expos = [jnp.exp(s - p).astype(bf16) for s, p in zip(scores, peaks)]
    sums = [dot(e, jnp.concatenate([halves(v, lane_k), ones], axis=-1)) for e, v in zip(expos, vs)]
    return [x[:, :TILE] for x in sums], [x[:, TILE:] for x in sums], peaks


def with_peak(num, peak):
    place = slot_lanes(num.shape[0])
    high = peak.astype(bf16).astype(f32)
    rest = peak - high
    mid = rest.astype(bf16).astype(f32)
    low = rest - mid
    num = jnp.where(place == HEAD + 1, high, num)
    num = jnp.where(place == HEAD + 2, mid, num)
    num = jnp.where(place == HEAD + 3, low, num)
    return num.astype(bf16)


def with_den(num, den):
    return jnp.where(slot_lanes(num.shape[0]) == HEAD, den, num)


def over_den(num):
    rows = num.shape[0]
    den = jnp.where(lanes(rows) < SLOT, num[:, HEAD : HEAD + 1], num[:, SLOT + HEAD : SLOT + HEAD + 1])
    return jnp.where(slot_lanes(rows) < HEAD, num / den, 0.0).astype(bf16)


def merge(part):
    count, rows = part.shape[0], part.shape[1]
    row = lax.broadcasted_iota(jnp.int32, (TILE, TILE), 0)
    col = lax.broadcasted_iota(jnp.int32, (TILE, TILE), 1)
    same = (row < SLOT) == (col < SLOT)
    place = jnp.where(row < SLOT, row, row - SLOT)
    pick = same & (place > HEAD) & (place < HEAD + 4)
    peaks = dot(part.reshape(count * rows, TILE), jnp.where(pick, 1.0, 0.0).astype(bf16))
    peaks = peaks.reshape(count, rows, TILE)
    peak = jnp.max(peaks, axis=0)
    total = jnp.sum(jnp.exp(peaks - peak[None]) * part.astype(f32), axis=0)
    return total, peak


def merge_tiles(value):
    return jnp.concatenate(
        [
            with_peak(*merge(value[:, :, at : at + TILE]))
            for at in range(0, value.shape[-1], TILE)
        ],
        axis=-1,
    )


def kernel(
    dims,
    tokens,
    visible,
    virtual,
    gains,
    w_time_qkv,
    w_time_o,
    w_read_q,
    w_read_kv,
    w_read_o,
    w_write_q,
    w_write_kv,
    w_write_o,
    w_up,
    w_down,
    v_up,
    v_down,
    track_out,
    virt_out,
    tok,
    x_recv,
    qkv,
    stage,
    y_recv,
    vis,
    vis_recv,
    time_bias,
    read_bias,
    y1t,
    y1,
    virt,
    vq,
    kv2,
    wq,
    pay,
    part,
    cross,
    vout,
    outv,
    raw,
    r_up,
    r_down,
    r_vup,
    r_vdown,
    p_time_qkv,
    p_time_o,
    p_read_q,
    p_read_kv,
    p_read_o,
    p_write_q,
    p_write_kv,
    p_write_o,
    load_sem,
    own_sem,
    vis_sem,
    tok_sem,
    back_sem,
    part_sem,
    cross_sem,
    gather_sem,
    out_sem,
):
    nfrm, nplane, chunks, per, frames, parts = dims
    trk, me = lax.axis_index("trk"), lax.axis_index("frm")
    spot, half = lax.div(trk, 2), lax.rem(trk, 2)
    width = HEADS * HEAD
    few = frames // parts
    owned = chunks * per
    keys = nfrm * frames
    tracks, virtuals = y1.shape[1], vq.shape[1]
    unit_rows = few * virtuals // nplane
    batch = owned // 2

    def column(k):
        return lax.rem(me + k, nfrm)

    def remote(src, dst, sems, where):
        return pltpu.make_async_remote_copy(
            src_ref=src,
            dst_ref=dst,
            send_sem=sems[0],
            recv_sem=sems[1],
            device_id=where,
            device_id_type=MESH,
        )

    def each(count, act):
        def body(k, carry):
            act(k)
            return carry

        lax.fori_loop(1, count, body, 0)

    weights = (w_time_qkv, w_time_o, w_read_q, w_read_kv, w_read_o, w_write_q, w_write_kv, w_write_o)
    offsets = []
    at = 0
    loads = []
    for n, w in enumerate(weights):
        cols = w.shape[1]
        offsets.append((at, cols))
        loads.append(pltpu.make_async_copy(w, raw.at[:, pl.ds(at, cols)], load_sem.at[n]))
        at += cols
    for w, dst in ((w_up, r_up), (w_down, r_down), (v_up, r_vup), (v_down, r_vdown), (virtual, virt), (tokens, tok)):
        loads.append(pltpu.make_async_copy(w, dst, load_sem.at[len(loads)]))
    loads.append(pltpu.make_async_copy(visible, vis, load_sem.at[len(loads)]))
    own = pltpu.make_async_copy(tokens.at[me], x_recv.at[me], own_sem)

    barrier = pltpu.get_barrier_semaphore()
    partner = (trk + 1 - 2 * half, me)
    pl.semaphore_signal(barrier, inc=1, device_id=partner, device_id_type=MESH)
    each(
        nfrm,
        lambda k: pl.semaphore_signal(barrier, inc=1, device_id=(trk, column(k)), device_id_type=MESH),
    )
    each(
        nplane,
        lambda i: pl.semaphore_signal(
            barrier, inc=1, device_id=(lax.rem(spot + i, nplane) * 2 + half, me), device_id_type=MESH
        ),
    )
    pl.semaphore_wait(barrier, nfrm - 1 + nplane - 1 + 1)

    def vis_copy(k):
        return remote(
            visible, vis_recv.at[me], (vis_sem.at[0, k], vis_sem.at[1, k]), (trk, column(k))
        )

    def tok_copy(c, k):
        return remote(
            tokens.at[column(k), pl.ds(c * per, per)],
            x_recv.at[me, pl.ds(c * per, per)],
            (tok_sem.at[0, c, k], tok_sem.at[1, c, k]),
            (trk, column(k)),
        )

    def back_copy(n, k):
        return remote(
            stage.at[n, column(k)],
            y_recv.at[n, me],
            (back_sem.at[0, n, k], back_sem.at[1, n, k]),
            (trk, column(k)),
        )

    each(nfrm, lambda k: vis_copy(k).start())
    for c in range(chunks):
        each(nfrm, lambda k: tok_copy(c, k).start())
    own.start()
    for load in loads:
        load.start()

    for load in loads:
        load.wait()
    cols_to = spread_matrix(False)
    rows_to = spread_matrix(True)

    def pad_cols(n, dst):
        start, cols = offsets[n]
        for b in range(cols // width):
            block = raw[:, start + b * width : start + (b + 1) * width]
            dst[:, b * WIDE : (b + 1) * WIDE] = dot(block, cols_to).astype(bf16)

    def pad_rows(n, dst):
        start, cols = offsets[n]
        dst[...] = dot(rows_to, raw[:, start : start + cols]).astype(bf16)

    pad_cols(0, p_time_qkv)
    pad_rows(1, p_time_o)
    pad_cols(2, p_read_q)
    pad_cols(3, p_read_kv)
    pad_rows(4, p_read_o)
    pad_cols(5, p_write_q)
    pad_cols(6, p_write_kv)
    pad_rows(7, p_write_o)

    for h in range(parts):
        rows = virt[h].reshape(few * virtuals, width).astype(f32)
        normed = (unit(rows) * gains[4:5, :]).astype(bf16)
        queries = dot(normed, p_read_q[...]).astype(bf16)
        vq[h * few : (h + 1) * few] = queries.reshape(few, virtuals, WIDE)

    flipped = (vis[...].astype(f32) - 1.0) * PENALTY
    read_bias[...] = jnp.concatenate([flipped, flipped], axis=-1)

    each(nfrm, lambda k: vis_copy(k).wait_recv())
    vis_recv[pl.ds(me, 1)] = vis[...][None]
    seen = [vis_recv[s].astype(f32) for s in range(nfrm)]
    seen = [s[h * few : (h + 1) * few] for h in range(parts) for s in seen]
    row = lax.broadcasted_iota(jnp.int32, (owned, tracks), 0)
    col = lax.broadcasted_iota(jnp.int32, (owned, tracks), 1)
    pick = jnp.where(col == row + me * owned, 1.0, 0.0).astype(bf16)
    time_bias[...] = (dot_t(pick, jnp.concatenate(seen, axis=0).astype(bf16)) - 1.0) * PENALTY
    own.wait()

    def project(c, carry):
        each(nfrm, lambda k: tok_copy(c, k).wait_recv())
        rows = []
        for t in range(per):
            blocks = [x_recv[s, c * per + t].astype(f32) for s in range(nfrm)]
            rows += [b[h * few : (h + 1) * few] for h in range(parts) for b in blocks]
        rows = jnp.concatenate(rows, axis=0)
        normed = (unit(rows) * gains[0:1, :]).astype(bf16)
        triple = dot(normed, p_time_qkv[...]).astype(bf16)
        qkv[pl.ds(c * per, per)] = triple.reshape(per, keys, 3 * WIDE)
        return carry

    lax.fori_loop(0, chunks, project, 0)
    asked = keys // parts

    def attend(n):
        h, first = n // 2, n % 2 * batch
        lane_k = lanes(keys)
        blocks = [(t, p) for t in range(batch) for p in range(PAIRS)]
        bias = [time_bias[first + t : first + t + 1, :] for t in range(batch)]
        bias = [jnp.concatenate([b, b], axis=-1) for b in bias]

        def piece(m, t, p):
            cols = slice(m * WIDE + p * TILE, m * WIDE + (p + 1) * TILE)
            if m == 0:
                return qkv[first + t, h * asked : (h + 1) * asked, cols]
            return qkv[first + t, :, cols]

        scores = [dot_t(piece(0, t, p), halves(piece(1, t, p), lane_k)) * SCALE + bias[t] for t, p in blocks]
        heads = [s[:, m * keys : (m + 1) * keys] for s in scores for m in range(2)]
        peaks = [jnp.max(s, axis=-1, keepdims=True) for s in heads]
        expos = [jnp.exp(s - m).astype(bf16) for s, m in zip(heads, peaks)]
        ones = sum_columns(keys)
        sums = [
            dot(
                jnp.concatenate(expos[2 * m : 2 * m + 2], axis=-1),
                jnp.concatenate([halves(piece(2, t, p), lane_k), ones], axis=-1),
            )
            for m, (t, p) in enumerate(blocks)
        ]
        tiles = [(x[:, :TILE] / x[:, TILE:]).astype(bf16) for x in sums]
        outs = [jnp.concatenate(tiles[t * PAIRS : (t + 1) * PAIRS], axis=-1) for t in range(batch)]
        projected = dot(jnp.concatenate(outs, axis=0), p_time_o[...])
        for s in range(nfrm):
            mine = [
                projected[t * asked + s * few : t * asked + (s + 1) * few] for t in range(batch)
            ]
            stage[n, s] = jnp.concatenate(mine, axis=0).astype(bf16)
        if n < 2:
            each(nfrm, lambda k: back_copy(n, k).start())
        y_recv[n, pl.ds(me, 1)] = stage[n, pl.ds(me, 1)]

    for n in range(2 * parts):
        attend(n)

    def send_back(n):
        each(nfrm, lambda k: back_copy(n, k).start())

    each(nfrm, lambda k: back_copy(0, k).wait_send())
    each(nfrm, lambda k: back_copy(1, k).wait_send())
    send_back(2)

    def add(h):
        for b in range(2):
            n = h * 2 + b
            each(nfrm, lambda k: back_copy(n, k).wait_recv())
            for o in range(nfrm):
                old = tok[o, b * batch : (b + 1) * batch].astype(f32)[:, h * few : (h + 1) * few]
                total = old + y_recv[n, o].astype(f32).reshape(batch, few, width)
                total = total.astype(bf16).astype(f32).reshape(batch * few, width)
                start = (o * owned + b * batch) * few
                for m in range(width // TILE):
                    y1t[m, start : start + batch * few, :] = total[:, m * TILE : (m + 1) * TILE]
        rows = []
        for f in range(few):
            rows.append(
                jnp.concatenate(
                    [y1t[m, pl.ds(f, tracks, stride=few), :] for m in range(width // TILE)], axis=-1
                )
            )
        rows = jnp.concatenate(rows, axis=0)
        span = slice(h * few, (h + 1) * few)
        y1[span] = rows.astype(bf16).reshape(few, tracks, width)
        normed = (unit(rows) * gains[1:2, :]).astype(bf16)
        kv2[span] = dot(normed, p_read_kv[...]).astype(bf16).reshape(few, tracks, 2 * WIDE)

    def write_queries(h):
        span = slice(h * few, (h + 1) * few)
        rows = y1[span].reshape(few * tracks, width).astype(f32)
        normed = (unit(rows) * gains[2:3, :]).astype(bf16)
        wq[span] = dot(normed, p_write_q[...]).astype(bf16).reshape(few, tracks, WIDE)

    def part_copy(h, i):
        other = lax.rem(spot + i, nplane)
        return remote(
            pay.at[h, other],
            part.at[h, spot],
            (part_sem.at[0, h, i], part_sem.at[1, h, i]),
            (other * 2 + half, me),
        )

    def across(h):
        return remote(
            cross.at[h, half], cross.at[h, half], (cross_sem.at[0, h], cross_sem.at[1, h]), partner
        )

    def gather_copy(h, i):
        return remote(
            vout.at[h, spot],
            vout.at[h, spot],
            (gather_sem.at[0, h, i], gather_sem.at[1, h, i]),
            (lax.rem(spot + i, nplane) * 2 + half, me),
        )

    def read(h):
        at = [p * TILE for p in range(PAIRS)]
        inside = range(h * few, (h + 1) * few)
        nums, dens, peaks = pair_attention(
            [vq[f, :, a : a + TILE] for f in inside for a in at],
            [kv2[f, :, a : a + TILE] for f in inside for a in at],
            [kv2[f, :, WIDE + a : WIDE + a + TILE] for f in inside for a in at],
            [read_bias[f : f + 1, :] for f in inside for a in at],
        )
        tiles = [with_peak(with_den(num, den), peak) for num, den, peak in zip(nums, dens, peaks)]
        for n in range(few):
            rows = jnp.concatenate(tiles[n * PAIRS : (n + 1) * PAIRS], axis=-1)
            for r in range(0, virtuals, unit_rows):
                u = (n * virtuals + r) // unit_rows
                pay[h, u] = rows[r : r + unit_rows]
        each(nplane, lambda i: part_copy(h, i).start())
        part[h, pl.ds(spot, 1)] = pay[h, pl.ds(spot, 1)]

    def cross_step(h):
        each(nplane, lambda i: part_copy(h, i).wait_recv())
        cross[h, pl.ds(half, 1)] = merge_tiles(part[h])[None]
        across(h).start()

    def virtual_step(h):
        across(h).wait_recv()
        both = cross[h]
        readout = jnp.concatenate(
            [over_den(merge(both[:, :, p * TILE : (p + 1) * TILE])[0]) for p in range(PAIRS)], axis=-1
        )
        virt1 = (virt[h, spot].astype(f32) + dot(readout, p_read_o[...])).astype(bf16).astype(f32)
        normed = (unit(virt1) * gains[5:6, :]).astype(bf16)
        middle = gelu(dot(normed, r_vup[...])).astype(bf16)
        vout[h, spot] = (virt1 + dot(middle, r_vdown[...])).astype(bf16)
        each(nplane, lambda i: gather_copy(h, i).start())

    def out_copy(at, group):
        span = pl.ds(at, group)
        return pltpu.make_async_copy(outv.at[span], track_out.at[span], out_sem.at[at])

    def write(h, g, group):
        if g == 0:
            each(nplane, lambda i: gather_copy(h, i).wait_recv())
        units = range(g * virtuals // unit_rows, (g + group) * virtuals // unit_rows)
        rows = jnp.concatenate([vout[h, u] for u in units], axis=0).astype(f32)
        normed = (unit(rows) * gains[6:7, :]).astype(bf16)
        pairs = dot(normed, p_write_kv[...]).astype(bf16)
        span = slice(h * few + g, h * few + g + group)
        at = [p * TILE for p in range(PAIRS)]
        blocks = [pairs[n * virtuals : (n + 1) * virtuals] for n in range(group)]
        nums, dens, _ = pair_attention(
            [wq[f, :, a : a + TILE] for f in range(span.start, span.stop) for a in at],
            [block[:, a : a + TILE] for block in blocks for a in at],
            [block[:, WIDE + a : WIDE + a + TILE] for block in blocks for a in at],
            None,
        )
        tiles = [(num / den).astype(bf16) for num, den in zip(nums, dens)]
        outs = [jnp.concatenate(tiles[n * PAIRS : (n + 1) * PAIRS], axis=-1) for n in range(group)]
        first = y1[span].reshape(group * tracks, width).astype(f32)
        second = first + dot(jnp.concatenate(outs, axis=0), p_write_o[...])
        second = second.astype(bf16).astype(f32)
        normed = (unit(second) * gains[3:4, :]).astype(bf16)
        middle = gelu(dot(normed, r_up[...])).astype(bf16)
        final = second + dot(middle, r_down[...])
        outv[span] = final.astype(bf16).reshape(group, tracks, width)
        out_copy(span.start, group).start()

    some = few // 2
    written = ((0, some), (some, few - some), (few, few))
    add(0)
    read(0)
    send_back(3)
    write_queries(0)
    cross_step(0)
    add(1)
    read(1)
    virtual_step(0)
    write_queries(1)
    cross_step(1)
    write(0, 0, some)
    virtual_step(1)
    write(0, some, few - some)
    write(1, 0, few)

    virt_done = pltpu.make_async_copy(vout, virt_out, own_sem)
    virt_done.start()

    each(nfrm, lambda k: vis_copy(k).wait_send())
    for c in range(chunks):
        each(nfrm, lambda k: tok_copy(c, k).wait_send())
    for n in range(2 * parts - 2, 2 * parts):
        each(nfrm, lambda k: back_copy(n, k).wait_send())
    for h in range(parts):
        each(nplane, lambda i: part_copy(h, i).wait_send())
        across(h).wait_send()
        each(nplane, lambda i: gather_copy(h, i).wait_send())
    for start, count in written:
        out_copy(start, count).wait()
    virt_done.wait()


def shards(tokens, visible, virtual, gains, *weights):
    tracks, frames, width = tokens.shape
    nfrm, nplane = lax.axis_size("frm"), lax.axis_size("trk") // 2
    virtuals = virtual.shape[1]
    owned = tracks // nfrm
    chunks, parts = 2, 2
    per = owned // chunks
    few = frames // parts
    unit_rows = few * virtuals // nplane
    hidden = weights[8].shape[1]
    keys = nfrm * frames
    dims = (nfrm, nplane, chunks, per, frames, parts)
    narrow = (nfrm, owned, frames, width)
    shares = (parts, nplane, unit_rows, width)
    vmem, anywhere = pl.BlockSpec(memory_space=pltpu.VMEM), pl.BlockSpec(memory_space=pl.ANY)
    dma = pltpu.SemaphoreType.DMA
    raw_cols = sum(w.shape[1] for w in weights[:8])
    track_out, virt_out = pl.pallas_call(
        functools.partial(kernel, dims),
        out_shape=(
            jax.ShapeDtypeStruct((frames, tracks, width), bf16),
            jax.ShapeDtypeStruct(shares, bf16),
        ),
        in_specs=[anywhere, anywhere, anywhere, vmem] + [anywhere] * 12,
        out_specs=(anywhere, anywhere),
        scratch_shapes=[
            pltpu.VMEM(narrow, bf16),
            pltpu.VMEM(narrow, bf16),
            pltpu.VMEM((owned, keys, 3 * WIDE), bf16),
            pltpu.VMEM((2 * parts, nfrm, owned // 2 * few, width), bf16),
            pltpu.VMEM((2 * parts, nfrm, owned // 2 * few, width), bf16),
            pltpu.VMEM((frames, tracks), jnp.int32),
            pltpu.VMEM((nfrm, frames, tracks), jnp.int32),
            pltpu.VMEM((owned, keys), f32),
            pltpu.VMEM((frames, 2 * tracks), f32),
            pltpu.VMEM((width // TILE, tracks * few, TILE), f32),
            pltpu.VMEM((frames, tracks, width), bf16),
            pltpu.VMEM(shares, bf16),
            pltpu.VMEM((frames, virtuals, WIDE), bf16),
            pltpu.VMEM((frames, tracks, 2 * WIDE), bf16),
            pltpu.VMEM((frames, tracks, WIDE), bf16),
            pltpu.VMEM((parts, nplane, unit_rows, WIDE), bf16),
            pltpu.VMEM((parts, nplane, unit_rows, WIDE), bf16),
            pltpu.VMEM((parts, 2, unit_rows, WIDE), bf16),
            pltpu.VMEM(shares, bf16),
            pltpu.VMEM((frames, tracks, width), bf16),
            pltpu.VMEM((width, raw_cols), bf16),
            pltpu.VMEM((width, hidden), bf16),
            pltpu.VMEM((hidden, width), bf16),
            pltpu.VMEM((width, hidden), bf16),
            pltpu.VMEM((hidden, width), bf16),
            pltpu.VMEM((width, 3 * WIDE), bf16),
            pltpu.VMEM((WIDE, width), bf16),
            pltpu.VMEM((width, WIDE), bf16),
            pltpu.VMEM((width, 2 * WIDE), bf16),
            pltpu.VMEM((WIDE, width), bf16),
            pltpu.VMEM((width, WIDE), bf16),
            pltpu.VMEM((width, 2 * WIDE), bf16),
            pltpu.VMEM((WIDE, width), bf16),
            dma((15,)),
            dma,
            dma((2, nfrm)),
            dma((2, chunks, nfrm)),
            dma((2, 2 * parts, nfrm)),
            dma((2, parts, nplane)),
            dma((2, parts)),
            dma((2, parts, nplane)),
            dma((frames,)),
        ],
        compiler_params=pltpu.CompilerParams(
            collective_id=0, has_side_effects=True, vmem_limit_bytes=56 * 1024 * 1024
        ),
    )(tokens.reshape(narrow), jnp.transpose(visible), virtual.reshape(shares), gains, *weights)
    return jnp.transpose(track_out, (1, 0, 2)), virt_out.reshape(frames, virtuals, width)


def solution(mesh):
    in_specs = (P("trk", "frm", None), P("trk", "frm"), P("frm", None, None)) + (P(),) * 13
    out_specs = (P("trk", "frm", None), P("frm", None, None))
    return jax.shard_map(shards, mesh=mesh, in_specs=in_specs, out_specs=out_specs, check_vma=False)
```

```python
import functools
import math

import jax
import jax.numpy as jnp
from jax import lax
from jax.experimental import pallas as pl
from jax.experimental.pallas import tpu as pltpu
from jax.sharding import PartitionSpec as P

HEADS = 8
HEAD = 48
SLOT = 64
TILE = 128
PAIRS = HEADS // 2
WIDE = HEADS * SLOT
PENALTY = 4.0
EPSILON = 1e-05
SCALE = 1.0 / math.sqrt(HEAD)
MESH = pl.DeviceIdType.MESH
f32 = jnp.float32
bf16 = jnp.bfloat16


def dot(a, b):
    return lax.dot_general(a, b, (((1,), (0,)), ((), ())), preferred_element_type=f32)


def dot_t(a, b):
    return lax.dot_general(a, b, (((1,), (1,)), ((), ())), preferred_element_type=f32)


def unit(x):
    center = x - jnp.mean(x, axis=-1, keepdims=True)
    spread = jnp.mean(center * center, axis=-1, keepdims=True)
    return center * lax.rsqrt(spread + EPSILON)


def gelu(x):
    return jax.nn.gelu(x, approximate=True)


def spread_matrix(rows_are_padded):
    shape = (WIDE, HEADS * HEAD) if rows_are_padded else (HEADS * HEAD, WIDE)
    tight = lax.broadcasted_iota(jnp.int32, shape, 1 if rows_are_padded else 0)
    padded = lax.broadcasted_iota(jnp.int32, shape, 0 if rows_are_padded else 1)
    target = tight
    for h in range(1, HEADS):
        target = target + jnp.where(tight >= HEAD * h, SLOT - HEAD, 0)
    return jnp.where(target == padded, 1.0, 0.0).astype(bf16)


def halves(x, lane):
    zero = jnp.zeros_like(x)
    return jnp.concatenate(
        [jnp.where(lane < SLOT, x, zero), jnp.where(lane < SLOT, zero, x)], axis=0
    )


def lanes(rows):
    return lax.broadcasted_iota(jnp.int32, (rows, TILE), 1)


def slot_lanes(rows):
    lane = lanes(rows)
    return jnp.where(lane < SLOT, lane, lane - SLOT)


def sum_columns(keys):
    row = lax.broadcasted_iota(jnp.int32, (2 * keys, TILE), 0)
    col = lax.broadcasted_iota(jnp.int32, (2 * keys, TILE), 1)
    return jnp.where((row < keys) == (col < SLOT), 1.0, 0.0).astype(bf16)


def pair_attention(qs, ks, vs, biases):
    keys = ks[0].shape[0]
    lane_k, lane_q = lanes(keys), lanes(qs[0].shape[0])
    ones = sum_columns(keys)
    scores = [dot_t(q, halves(k, lane_k)) * SCALE for q, k in zip(qs, ks)]
    if biases is not None:
        scores = [s + b for s, b in zip(scores, biases)]
    left = lane_q < SLOT
    first = [jnp.max(jnp.where(left, s, -jnp.inf), axis=-1, keepdims=True) for s in scores]
    second = [jnp.max(jnp.where(left, -jnp.inf, s), axis=-1, keepdims=True) for s in scores]
    peaks = [jnp.where(left, x, y) for x, y in zip(first, second)]
    expos = [jnp.exp(s - p).astype(bf16) for s, p in zip(scores, peaks)]
    sums = [dot(e, jnp.concatenate([halves(v, lane_k), ones], axis=-1)) for e, v in zip(expos, vs)]
    return [x[:, :TILE] for x in sums], [x[:, TILE:] for x in sums], peaks


def with_peak(num, peak):
    place = slot_lanes(num.shape[0])
    high = peak.astype(bf16).astype(f32)
    rest = peak - high
    mid = rest.astype(bf16).astype(f32)
    low = rest - mid
    num = jnp.where(place == HEAD + 1, high, num)
    num = jnp.where(place == HEAD + 2, mid, num)
    num = jnp.where(place == HEAD + 3, low, num)
    return num.astype(bf16)


def with_den(num, den):
    return jnp.where(slot_lanes(num.shape[0]) == HEAD, den, num)


def over_den(num):
    rows = num.shape[0]
    den = jnp.where(lanes(rows) < SLOT, num[:, HEAD : HEAD + 1], num[:, SLOT + HEAD : SLOT + HEAD + 1])
    return jnp.where(slot_lanes(rows) < HEAD, num / den, 0.0).astype(bf16)


def merge(part):
    count, rows = part.shape[0], part.shape[1]
    row = lax.broadcasted_iota(jnp.int32, (TILE, TILE), 0)
    col = lax.broadcasted_iota(jnp.int32, (TILE, TILE), 1)
    same = (row < SLOT) == (col < SLOT)
    place = jnp.where(row < SLOT, row, row - SLOT)
    pick = same & (place > HEAD) & (place < HEAD + 4)
    peaks = dot(part.reshape(count * rows, TILE), jnp.where(pick, 1.0, 0.0).astype(bf16))
    peaks = peaks.reshape(count, rows, TILE)
    peak = jnp.max(peaks, axis=0)
    total = jnp.sum(jnp.exp(peaks - peak[None]) * part.astype(f32), axis=0)
    return total, peak


def merge_tiles(value):
    return jnp.concatenate(
        [
            with_peak(*merge(value[:, :, at : at + TILE]))
            for at in range(0, value.shape[-1], TILE)
        ],
        axis=-1,
    )


def kernel(
    dims,
    tokens,
    visible,
    virtual,
    gains,
    w_time_qkv,
    w_time_o,
    w_read_q,
    w_read_kv,
    w_read_o,
    w_write_q,
    w_write_kv,
    w_write_o,
    w_up,
    w_down,
    v_up,
    v_down,
    track_out,
    virt_out,
    tok,
    x_recv,
    qkv,
    stage,
    y_recv,
    vis,
    vis_recv,
    time_bias,
    read_bias,
    y1t,
    y1,
    virt,
    vq,
    kv2,
    wq,
    pay,
    part,
    cross,
    vout,
    outv,
    raw,
    r_up,
    r_down,
    r_vup,
    r_vdown,
    p_time_qkv,
    p_time_o,
    p_read_q,
    p_read_kv,
    p_read_o,
    p_write_q,
    p_write_kv,
    p_write_o,
    load_sem,
    own_sem,
    vis_sem,
    tok_sem,
    back_sem,
    part_sem,
    cross_sem,
    gather_sem,
    out_sem,
):
    nfrm, nplane, chunks, per, frames, parts = dims
    trk, me = lax.axis_index("trk"), lax.axis_index("frm")
    spot, half = lax.div(trk, 2), lax.rem(trk, 2)
    width = HEADS * HEAD
    few = frames // parts
    owned = chunks * per
    keys = nfrm * frames
    tracks, virtuals = y1.shape[1], vq.shape[1]
    unit_rows = few * virtuals // nplane
    batch = owned // 2

    def column(k):
        return lax.rem(me + k, nfrm)

    def remote(src, dst, sems, where):
        return pltpu.make_async_remote_copy(
            src_ref=src,
            dst_ref=dst,
            send_sem=sems[0],
            recv_sem=sems[1],
            device_id=where,
            device_id_type=MESH,
        )

    def each(count, act):
        def body(k, carry):
            act(k)
            return carry

        lax.fori_loop(1, count, body, 0)

    weights = (w_time_qkv, w_time_o, w_read_q, w_read_kv, w_read_o, w_write_q, w_write_kv, w_write_o)
    offsets = []
    at = 0
    loads = []
    for n, w in enumerate(weights):
        cols = w.shape[1]
        offsets.append((at, cols))
        loads.append(pltpu.make_async_copy(w, raw.at[:, pl.ds(at, cols)], load_sem.at[n]))
        at += cols
    for w, dst in ((w_up, r_up), (w_down, r_down), (v_up, r_vup), (v_down, r_vdown), (virtual, virt), (tokens, tok)):
        loads.append(pltpu.make_async_copy(w, dst, load_sem.at[len(loads)]))
    loads.append(pltpu.make_async_copy(visible, vis, load_sem.at[len(loads)]))
    own = pltpu.make_async_copy(tokens.at[me], x_recv.at[me], own_sem)

    barrier = pltpu.get_barrier_semaphore()
    partner = (trk + 1 - 2 * half, me)
    pl.semaphore_signal(barrier, inc=1, device_id=partner, device_id_type=MESH)
    each(
        nfrm,
        lambda k: pl.semaphore_signal(barrier, inc=1, device_id=(trk, column(k)), device_id_type=MESH),
    )
    each(
        nplane,
        lambda i: pl.semaphore_signal(
            barrier, inc=1, device_id=(lax.rem(spot + i, nplane) * 2 + half, me), device_id_type=MESH
        ),
    )
    pl.semaphore_wait(barrier, nfrm - 1 + nplane - 1 + 1)

    def vis_copy(k):
        return remote(
            visible, vis_recv.at[me], (vis_sem.at[0, k], vis_sem.at[1, k]), (trk, column(k))
        )

    def tok_copy(c, k):
        return remote(
            tokens.at[column(k), pl.ds(c * per, per)],
            x_recv.at[me, pl.ds(c * per, per)],
            (tok_sem.at[0, c, k], tok_sem.at[1, c, k]),
            (trk, column(k)),
        )

    def back_copy(n, k):
        return remote(
            stage.at[n, column(k)],
            y_recv.at[n, me],
            (back_sem.at[0, n, k], back_sem.at[1, n, k]),
            (trk, column(k)),
        )

    each(nfrm, lambda k: vis_copy(k).start())
    for c in range(chunks):
        each(nfrm, lambda k: tok_copy(c, k).start())
    own.start()
    for load in loads:
        load.start()

    for load in loads:
        load.wait()
    cols_to = spread_matrix(False)
    rows_to = spread_matrix(True)

    def pad_cols(n, dst):
        start, cols = offsets[n]
        for b in range(cols // width):
            block = raw[:, start + b * width : start + (b + 1) * width]
            dst[:, b * WIDE : (b + 1) * WIDE] = dot(block, cols_to).astype(bf16)

    def pad_rows(n, dst):
        start, cols = offsets[n]
        dst[...] = dot(rows_to, raw[:, start : start + cols]).astype(bf16)

    pad_cols(0, p_time_qkv)
    pad_rows(1, p_time_o)
    pad_cols(2, p_read_q)
    pad_cols(3, p_read_kv)
    pad_rows(4, p_read_o)
    pad_cols(5, p_write_q)
    pad_cols(6, p_write_kv)
    pad_rows(7, p_write_o)

    for h in range(parts):
        rows = virt[h].reshape(few * virtuals, width).astype(f32)
        normed = (unit(rows) * gains[4:5, :]).astype(bf16)
        queries = dot(normed, p_read_q[...]).astype(bf16)
        vq[h * few : (h + 1) * few] = queries.reshape(few, virtuals, WIDE)

    flipped = (vis[...].astype(f32) - 1.0) * PENALTY
    read_bias[...] = jnp.concatenate([flipped, flipped], axis=-1)

    each(nfrm, lambda k: vis_copy(k).wait_recv())
    vis_recv[pl.ds(me, 1)] = vis[...][None]
    seen = [vis_recv[s].astype(f32) for s in range(nfrm)]
    seen = [s[h * few : (h + 1) * few] for h in range(parts) for s in seen]
    row = lax.broadcasted_iota(jnp.int32, (owned, tracks), 0)
    col = lax.broadcasted_iota(jnp.int32, (owned, tracks), 1)
    pick = jnp.where(col == row + me * owned, 1.0, 0.0).astype(bf16)
    time_bias[...] = (dot_t(pick, jnp.concatenate(seen, axis=0).astype(bf16)) - 1.0) * PENALTY
    own.wait()

    def project(c, carry):
        each(nfrm, lambda k: tok_copy(c, k).wait_recv())
        rows = []
        for t in range(per):
            blocks = [x_recv[s, c * per + t].astype(f32) for s in range(nfrm)]
            rows += [b[h * few : (h + 1) * few] for h in range(parts) for b in blocks]
        rows = jnp.concatenate(rows, axis=0)
        normed = (unit(rows) * gains[0:1, :]).astype(bf16)
        triple = dot(normed, p_time_qkv[...]).astype(bf16)
        qkv[pl.ds(c * per, per)] = triple.reshape(per, keys, 3 * WIDE)
        return carry

    lax.fori_loop(0, chunks, project, 0)
    asked = keys // parts

    def attend(n):
        h, first = n // 2, n % 2 * batch
        lane_k = lanes(keys)
        blocks = [(t, p) for t in range(batch) for p in range(PAIRS)]
        bias = [time_bias[first + t : first + t + 1, :] for t in range(batch)]
        bias = [jnp.concatenate([b, b], axis=-1) for b in bias]

        def piece(m, t, p):
            cols = slice(m * WIDE + p * TILE, m * WIDE + (p + 1) * TILE)
            if m == 0:
                return qkv[first + t, h * asked : (h + 1) * asked, cols]
            return qkv[first + t, :, cols]

        scores = [dot_t(piece(0, t, p), halves(piece(1, t, p), lane_k)) * SCALE + bias[t] for t, p in blocks]
        heads = [s[:, m * keys : (m + 1) * keys] for s in scores for m in range(2)]
        peaks = [jnp.max(s, axis=-1, keepdims=True) for s in heads]
        expos = [jnp.exp(s - m).astype(bf16) for s, m in zip(heads, peaks)]
        ones = sum_columns(keys)
        sums = [
            dot(
                jnp.concatenate(expos[2 * m : 2 * m + 2], axis=-1),
                jnp.concatenate([halves(piece(2, t, p), lane_k), ones], axis=-1),
            )
            for m, (t, p) in enumerate(blocks)
        ]
        tiles = [(x[:, :TILE] / x[:, TILE:]).astype(bf16) for x in sums]
        outs = [jnp.concatenate(tiles[t * PAIRS : (t + 1) * PAIRS], axis=-1) for t in range(batch)]
        projected = dot(jnp.concatenate(outs, axis=0), p_time_o[...])
        for s in range(nfrm):
            mine = [
                projected[t * asked + s * few : t * asked + (s + 1) * few] for t in range(batch)
            ]
            stage[n, s] = jnp.concatenate(mine, axis=0).astype(bf16)
        if n < 2:
            each(nfrm, lambda k: back_copy(n, k).start())
        y_recv[n, pl.ds(me, 1)] = stage[n, pl.ds(me, 1)]

    for n in range(2 * parts):
        attend(n)

    def send_back(n):
        each(nfrm, lambda k: back_copy(n, k).start())

    def next_part(h):
        for n in (2 * h - 2, 2 * h - 1):
            each(nfrm, lambda k: back_copy(n, k).wait_send())
        send_back(2 * h)
        send_back(2 * h + 1)

    next_part(1)

    def add(h):
        for b in range(2):
            n = h * 2 + b
            each(nfrm, lambda k: back_copy(n, k).wait_recv())
            for o in range(nfrm):
                old = tok[o, b * batch : (b + 1) * batch].astype(f32)[:, h * few : (h + 1) * few]
                total = old + y_recv[n, o].astype(f32).reshape(batch, few, width)
                total = total.astype(bf16).astype(f32).reshape(batch * few, width)
                start = (o * owned + b * batch) * few
                for m in range(width // TILE):
                    y1t[m, start : start + batch * few, :] = total[:, m * TILE : (m + 1) * TILE]
        rows = []
        for f in range(few):
            rows.append(
                jnp.concatenate(
                    [y1t[m, pl.ds(f, tracks, stride=few), :] for m in range(width // TILE)], axis=-1
                )
            )
        rows = jnp.concatenate(rows, axis=0)
        span = slice(h * few, (h + 1) * few)
        y1[span] = rows.astype(bf16).reshape(few, tracks, width)
        normed = (unit(rows) * gains[1:2, :]).astype(bf16)
        kv2[span] = dot(normed, p_read_kv[...]).astype(bf16).reshape(few, tracks, 2 * WIDE)

    def write_queries(h):
        span = slice(h * few, (h + 1) * few)
        rows = y1[span].reshape(few * tracks, width).astype(f32)
        normed = (unit(rows) * gains[2:3, :]).astype(bf16)
        wq[span] = dot(normed, p_write_q[...]).astype(bf16).reshape(few, tracks, WIDE)

    def part_copy(h, i):
        other = lax.rem(spot + i, nplane)
        return remote(
            pay.at[h, other],
            part.at[h, spot],
            (part_sem.at[0, h, i], part_sem.at[1, h, i]),
            (other * 2 + half, me),
        )

    def across(h):
        return remote(
            cross.at[h, half], cross.at[h, half], (cross_sem.at[0, h], cross_sem.at[1, h]), partner
        )

    def gather_copy(h, i):
        return remote(
            vout.at[h, spot],
            vout.at[h, spot],
            (gather_sem.at[0, h, i], gather_sem.at[1, h, i]),
            (lax.rem(spot + i, nplane) * 2 + half, me),
        )

    def read(h):
        at = [p * TILE for p in range(PAIRS)]
        inside = range(h * few, (h + 1) * few)
        nums, dens, peaks = pair_attention(
            [vq[f, :, a : a + TILE] for f in inside for a in at],
            [kv2[f, :, a : a + TILE] for f in inside for a in at],
            [kv2[f, :, WIDE + a : WIDE + a + TILE] for f in inside for a in at],
            [read_bias[f : f + 1, :] for f in inside for a in at],
        )
        tiles = [with_peak(with_den(num, den), peak) for num, den, peak in zip(nums, dens, peaks)]
        for n in range(few):
            rows = jnp.concatenate(tiles[n * PAIRS : (n + 1) * PAIRS], axis=-1)
            for r in range(0, virtuals, unit_rows):
                u = (n * virtuals + r) // unit_rows
                pay[h, u] = rows[r : r + unit_rows]
        each(nplane, lambda i: part_copy(h, i).start())
        part[h, pl.ds(spot, 1)] = pay[h, pl.ds(spot, 1)]

    def cross_step(h):
        each(nplane, lambda i: part_copy(h, i).wait_recv())
        cross[h, pl.ds(half, 1)] = merge_tiles(part[h])[None]
        across(h).start()

    def virtual_step(h):
        across(h).wait_recv()
        both = cross[h]
        readout = jnp.concatenate(
            [over_den(merge(both[:, :, p * TILE : (p + 1) * TILE])[0]) for p in range(PAIRS)], axis=-1
        )
        virt1 = (virt[h, spot].astype(f32) + dot(readout, p_read_o[...])).astype(bf16).astype(f32)
        normed = (unit(virt1) * gains[5:6, :]).astype(bf16)
        middle = gelu(dot(normed, r_vup[...])).astype(bf16)
        vout[h, spot] = (virt1 + dot(middle, r_vdown[...])).astype(bf16)
        each(nplane, lambda i: gather_copy(h, i).start())

    def out_copy(at, group):
        span = pl.ds(at, group)
        return pltpu.make_async_copy(outv.at[span], track_out.at[span], out_sem.at[at])

    def write(h, g, group):
        if g == 0:
            each(nplane, lambda i: gather_copy(h, i).wait_recv())
        units = range(g * virtuals // unit_rows, (g + group) * virtuals // unit_rows)
        rows = jnp.concatenate([vout[h, u] for u in units], axis=0).astype(f32)
        normed = (unit(rows) * gains[6:7, :]).astype(bf16)
        pairs = dot(normed, p_write_kv[...]).astype(bf16)
        span = slice(h * few + g, h * few + g + group)
        at = [p * TILE for p in range(PAIRS)]
        blocks = [pairs[n * virtuals : (n + 1) * virtuals] for n in range(group)]
        nums, dens, _ = pair_attention(
            [wq[f, :, a : a + TILE] for f in range(span.start, span.stop) for a in at],
            [block[:, a : a + TILE] for block in blocks for a in at],
            [block[:, WIDE + a : WIDE + a + TILE] for block in blocks for a in at],
            None,
        )
        tiles = [(num / den).astype(bf16) for num, den in zip(nums, dens)]
        outs = [jnp.concatenate(tiles[n * PAIRS : (n + 1) * PAIRS], axis=-1) for n in range(group)]
        first = y1[span].reshape(group * tracks, width).astype(f32)
        second = first + dot(jnp.concatenate(outs, axis=0), p_write_o[...])
        second = second.astype(bf16).astype(f32)
        normed = (unit(second) * gains[3:4, :]).astype(bf16)
        middle = gelu(dot(normed, r_up[...])).astype(bf16)
        final = second + dot(middle, r_down[...])
        outv[span] = final.astype(bf16).reshape(group, tracks, width)
        out_copy(span.start, group).start()

    written = [(h * few, few) for h in range(parts)]
    add(0)
    read(0)
    next_part(2)
    write_queries(0)
    add(1)
    read(1)
    next_part(3)
    cross_step(0)
    write_queries(1)
    add(2)
    read(2)
    cross_step(1)
    virtual_step(0)
    write_queries(2)
    add(3)
    read(3)
    cross_step(2)
    virtual_step(1)
    write_queries(3)
    write(0, 0, few)
    cross_step(3)
    virtual_step(2)
    write(1, 0, few)
    virtual_step(3)
    write(2, 0, few)
    write(3, 0, few)

    virt_done = pltpu.make_async_copy(vout, virt_out, own_sem)
    virt_done.start()

    each(nfrm, lambda k: vis_copy(k).wait_send())
    for c in range(chunks):
        each(nfrm, lambda k: tok_copy(c, k).wait_send())
    for n in range(2 * parts - 2, 2 * parts):
        each(nfrm, lambda k: back_copy(n, k).wait_send())
    for h in range(parts):
        each(nplane, lambda i: part_copy(h, i).wait_send())
        across(h).wait_send()
        each(nplane, lambda i: gather_copy(h, i).wait_send())
    for start, count in written:
        out_copy(start, count).wait()
    virt_done.wait()


def shards(tokens, visible, virtual, gains, *weights):
    tracks, frames, width = tokens.shape
    nfrm, nplane = lax.axis_size("frm"), lax.axis_size("trk") // 2
    virtuals = virtual.shape[1]
    owned = tracks // nfrm
    chunks, parts = 2, 4
    per = owned // chunks
    few = frames // parts
    unit_rows = few * virtuals // nplane
    hidden = weights[8].shape[1]
    keys = nfrm * frames
    dims = (nfrm, nplane, chunks, per, frames, parts)
    narrow = (nfrm, owned, frames, width)
    shares = (parts, nplane, unit_rows, width)
    vmem, anywhere = pl.BlockSpec(memory_space=pltpu.VMEM), pl.BlockSpec(memory_space=pl.ANY)
    dma = pltpu.SemaphoreType.DMA
    raw_cols = sum(w.shape[1] for w in weights[:8])
    track_out, virt_out = pl.pallas_call(
        functools.partial(kernel, dims),
        out_shape=(
            jax.ShapeDtypeStruct((frames, tracks, width), bf16),
            jax.ShapeDtypeStruct(shares, bf16),
        ),
        in_specs=[anywhere, anywhere, anywhere, vmem] + [anywhere] * 12,
        out_specs=(anywhere, anywhere),
        scratch_shapes=[
            pltpu.VMEM(narrow, bf16),
            pltpu.VMEM(narrow, bf16),
            pltpu.VMEM((owned, keys, 3 * WIDE), bf16),
            pltpu.VMEM((2 * parts, nfrm, owned // 2 * few, width), bf16),
            pltpu.VMEM((2 * parts, nfrm, owned // 2 * few, width), bf16),
            pltpu.VMEM((frames, tracks), jnp.int32),
            pltpu.VMEM((nfrm, frames, tracks), jnp.int32),
            pltpu.VMEM((owned, keys), f32),
            pltpu.VMEM((frames, 2 * tracks), f32),
            pltpu.VMEM((width // TILE, tracks * few, TILE), f32),
            pltpu.VMEM((frames, tracks, width), bf16),
            pltpu.VMEM(shares, bf16),
            pltpu.VMEM((frames, virtuals, WIDE), bf16),
            pltpu.VMEM((frames, tracks, 2 * WIDE), bf16),
            pltpu.VMEM((frames, tracks, WIDE), bf16),
            pltpu.VMEM((parts, nplane, unit_rows, WIDE), bf16),
            pltpu.VMEM((parts, nplane, unit_rows, WIDE), bf16),
            pltpu.VMEM((parts, 2, unit_rows, WIDE), bf16),
            pltpu.VMEM(shares, bf16),
            pltpu.VMEM((frames, tracks, width), bf16),
            pltpu.VMEM((width, raw_cols), bf16),
            pltpu.VMEM((width, hidden), bf16),
            pltpu.VMEM((hidden, width), bf16),
            pltpu.VMEM((width, hidden), bf16),
            pltpu.VMEM((hidden, width), bf16),
            pltpu.VMEM((width, 3 * WIDE), bf16),
            pltpu.VMEM((WIDE, width), bf16),
            pltpu.VMEM((width, WIDE), bf16),
            pltpu.VMEM((width, 2 * WIDE), bf16),
            pltpu.VMEM((WIDE, width), bf16),
            pltpu.VMEM((width, WIDE), bf16),
            pltpu.VMEM((width, 2 * WIDE), bf16),
            pltpu.VMEM((WIDE, width), bf16),
            dma((15,)),
            dma,
            dma((2, nfrm)),
            dma((2, chunks, nfrm)),
            dma((2, 2 * parts, nfrm)),
            dma((2, parts, nplane)),
            dma((2, parts)),
            dma((2, parts, nplane)),
            dma((frames,)),
        ],
        compiler_params=pltpu.CompilerParams(
            collective_id=0, has_side_effects=True, vmem_limit_bytes=56 * 1024 * 1024
        ),
    )(tokens.reshape(narrow), jnp.transpose(visible), virtual.reshape(shares), gains, *weights)
    return jnp.transpose(track_out, (1, 0, 2)), virt_out.reshape(frames, virtuals, width)


def solution(mesh):
    in_specs = (P("trk", "frm", None), P("trk", "frm"), P("frm", None, None)) + (P(),) * 13
    out_specs = (P("trk", "frm", None), P("frm", None, None))
    return jax.shard_map(shards, mesh=mesh, in_specs=in_specs, out_specs=out_specs, check_vma=False)
```

```python
import functools
import math

import jax
import jax.numpy as jnp
from jax import lax
from jax.experimental import pallas as pl
from jax.experimental.pallas import tpu as pltpu
from jax.sharding import PartitionSpec as P

HEADS = 8
HEAD = 48
SLOT = 64
TILE = 128
PAIRS = HEADS // 2
WIDE = HEADS * SLOT
PENALTY = 4.0
EPSILON = 1e-05
SCALE = 1.0 / math.sqrt(HEAD)
MESH = pl.DeviceIdType.MESH
f32 = jnp.float32
bf16 = jnp.bfloat16


def dot(a, b):
    return lax.dot_general(a, b, (((1,), (0,)), ((), ())), preferred_element_type=f32)


def dot_t(a, b):
    return lax.dot_general(a, b, (((1,), (1,)), ((), ())), preferred_element_type=f32)


def unit(x):
    center = x - jnp.mean(x, axis=-1, keepdims=True)
    spread = jnp.mean(center * center, axis=-1, keepdims=True)
    return center * lax.rsqrt(spread + EPSILON)


def gelu(x):
    return jax.nn.gelu(x, approximate=True)


def spread_matrix(rows_are_padded):
    shape = (WIDE, HEADS * HEAD) if rows_are_padded else (HEADS * HEAD, WIDE)
    tight = lax.broadcasted_iota(jnp.int32, shape, 1 if rows_are_padded else 0)
    padded = lax.broadcasted_iota(jnp.int32, shape, 0 if rows_are_padded else 1)
    target = tight
    for h in range(1, HEADS):
        target = target + jnp.where(tight >= HEAD * h, SLOT - HEAD, 0)
    return jnp.where(target == padded, 1.0, 0.0).astype(bf16)


def halves(x, lane):
    zero = jnp.zeros_like(x)
    return jnp.concatenate(
        [jnp.where(lane < SLOT, x, zero), jnp.where(lane < SLOT, zero, x)], axis=0
    )


def lanes(rows):
    return lax.broadcasted_iota(jnp.int32, (rows, TILE), 1)


def slot_lanes(rows):
    lane = lanes(rows)
    return jnp.where(lane < SLOT, lane, lane - SLOT)


def sum_columns(keys):
    row = lax.broadcasted_iota(jnp.int32, (2 * keys, TILE), 0)
    col = lax.broadcasted_iota(jnp.int32, (2 * keys, TILE), 1)
    return jnp.where((row < keys) == (col < SLOT), 1.0, 0.0).astype(bf16)


def pair_attention(qs, ks, vs, biases):
    keys = ks[0].shape[0]
    lane_k, lane_q = lanes(keys), lanes(qs[0].shape[0])
    ones = sum_columns(keys)
    scores = [dot_t(q, halves(k, lane_k)) * SCALE for q, k in zip(qs, ks)]
    if biases is not None:
        scores = [s + b for s, b in zip(scores, biases)]
    left = lane_q < SLOT
    first = [jnp.max(jnp.where(left, s, -jnp.inf), axis=-1, keepdims=True) for s in scores]
    second = [jnp.max(jnp.where(left, -jnp.inf, s), axis=-1, keepdims=True) for s in scores]
    peaks = [jnp.where(left, x, y) for x, y in zip(first, second)]
    expos = [jnp.exp(s - p).astype(bf16) for s, p in zip(scores, peaks)]
    sums = [dot(e, jnp.concatenate([halves(v, lane_k), ones], axis=-1)) for e, v in zip(expos, vs)]
    return [x[:, :TILE] for x in sums], [x[:, TILE:] for x in sums], peaks


def with_peak(num, peak):
    place = slot_lanes(num.shape[0])
    high = peak.astype(bf16).astype(f32)
    rest = peak - high
    mid = rest.astype(bf16).astype(f32)
    low = rest - mid
    num = jnp.where(place == HEAD + 1, high, num)
    num = jnp.where(place == HEAD + 2, mid, num)
    num = jnp.where(place == HEAD + 3, low, num)
    return num.astype(bf16)


def with_den(num, den):
    return jnp.where(slot_lanes(num.shape[0]) == HEAD, den, num)


def over_den(num):
    rows = num.shape[0]
    den = jnp.where(lanes(rows) < SLOT, num[:, HEAD : HEAD + 1], num[:, SLOT + HEAD : SLOT + HEAD + 1])
    return jnp.where(slot_lanes(rows) < HEAD, num / den, 0.0).astype(bf16)


def merge(part):
    count, rows = part.shape[0], part.shape[1]
    row = lax.broadcasted_iota(jnp.int32, (TILE, TILE), 0)
    col = lax.broadcasted_iota(jnp.int32, (TILE, TILE), 1)
    same = (row < SLOT) == (col < SLOT)
    place = jnp.where(row < SLOT, row, row - SLOT)
    pick = same & (place > HEAD) & (place < HEAD + 4)
    peaks = dot(part.reshape(count * rows, TILE), jnp.where(pick, 1.0, 0.0).astype(bf16))
    peaks = peaks.reshape(count, rows, TILE)
    peak = jnp.max(peaks, axis=0)
    total = jnp.sum(jnp.exp(peaks - peak[None]) * part.astype(f32), axis=0)
    return total, peak


def merge_tiles(value):
    return jnp.concatenate(
        [
            with_peak(*merge(value[:, :, at : at + TILE]))
            for at in range(0, value.shape[-1], TILE)
        ],
        axis=-1,
    )


def kernel(
    dims,
    tokens,
    visible,
    virtual,
    gains,
    w_time_qkv,
    w_time_o,
    w_read_q,
    w_read_kv,
    w_read_o,
    w_write_q,
    w_write_kv,
    w_write_o,
    w_up,
    w_down,
    v_up,
    v_down,
    track_out,
    virt_out,
    tok,
    x_recv,
    qkv,
    stage,
    y_recv,
    vis,
    vis_recv,
    time_bias,
    read_bias,
    y1t,
    y1,
    virt,
    vq,
    kv2,
    wq,
    pay,
    part,
    cross,
    vout,
    outv,
    raw,
    r_up,
    r_down,
    r_vup,
    r_vdown,
    p_time_qkv,
    p_time_o,
    p_read_q,
    p_read_kv,
    p_read_o,
    p_write_q,
    p_write_kv,
    p_write_o,
    load_sem,
    own_sem,
    vis_sem,
    tok_sem,
    back_sem,
    part_sem,
    cross_sem,
    gather_sem,
    out_sem,
):
    nfrm, nplane, chunks, per, frames, parts = dims
    trk, me = lax.axis_index("trk"), lax.axis_index("frm")
    spot, half = lax.div(trk, 2), lax.rem(trk, 2)
    width = HEADS * HEAD
    few = frames // parts
    owned = chunks * per
    keys = nfrm * frames
    tracks, virtuals = y1.shape[1], vq.shape[1]
    unit_rows = few * virtuals // nplane
    batch = owned // 2

    def column(k):
        return lax.rem(me + k, nfrm)

    def remote(src, dst, sems, where):
        return pltpu.make_async_remote_copy(
            src_ref=src,
            dst_ref=dst,
            send_sem=sems[0],
            recv_sem=sems[1],
            device_id=where,
            device_id_type=MESH,
        )

    def each(count, act):
        def body(k, carry):
            act(k)
            return carry

        lax.fori_loop(1, count, body, 0)

    weights = (w_time_qkv, w_time_o, w_read_q, w_read_kv, w_read_o, w_write_q, w_write_kv, w_write_o)
    offsets = []
    at = 0
    loads = []
    for n, w in enumerate(weights):
        cols = w.shape[1]
        offsets.append((at, cols))
        loads.append(pltpu.make_async_copy(w, raw.at[:, pl.ds(at, cols)], load_sem.at[n]))
        at += cols
    for w, dst in ((w_up, r_up), (w_down, r_down), (v_up, r_vup), (v_down, r_vdown), (virtual, virt), (tokens, tok)):
        loads.append(pltpu.make_async_copy(w, dst, load_sem.at[len(loads)]))
    loads.append(pltpu.make_async_copy(visible, vis, load_sem.at[len(loads)]))
    own = pltpu.make_async_copy(tokens.at[me], x_recv.at[me], own_sem)

    barrier = pltpu.get_barrier_semaphore()
    partner = (trk + 1 - 2 * half, me)
    pl.semaphore_signal(barrier, inc=1, device_id=partner, device_id_type=MESH)
    each(
        nfrm,
        lambda k: pl.semaphore_signal(barrier, inc=1, device_id=(trk, column(k)), device_id_type=MESH),
    )
    each(
        nplane,
        lambda i: pl.semaphore_signal(
            barrier, inc=1, device_id=(lax.rem(spot + i, nplane) * 2 + half, me), device_id_type=MESH
        ),
    )
    pl.semaphore_wait(barrier, nfrm - 1 + nplane - 1 + 1)

    def vis_copy(k):
        return remote(
            visible, vis_recv.at[me], (vis_sem.at[0, k], vis_sem.at[1, k]), (trk, column(k))
        )

    def tok_copy(c, k):
        return remote(
            tokens.at[column(k), pl.ds(c * per, per)],
            x_recv.at[me, pl.ds(c * per, per)],
            (tok_sem.at[0, c, k], tok_sem.at[1, c, k]),
            (trk, column(k)),
        )

    def back_copy(n, k):
        return remote(
            stage.at[n, column(k)],
            y_recv.at[n, me],
            (back_sem.at[0, n, k], back_sem.at[1, n, k]),
            (trk, column(k)),
        )

    each(nfrm, lambda k: vis_copy(k).start())
    for c in range(chunks):
        each(nfrm, lambda k: tok_copy(c, k).start())
    own.start()
    for load in loads:
        load.start()

    for load in loads:
        load.wait()
    cols_to = spread_matrix(False)
    rows_to = spread_matrix(True)

    def pad_cols(n, dst):
        start, cols = offsets[n]
        for b in range(cols // width):
            block = raw[:, start + b * width : start + (b + 1) * width]
            dst[:, b * WIDE : (b + 1) * WIDE] = dot(block, cols_to).astype(bf16)

    def pad_rows(n, dst):
        start, cols = offsets[n]
        dst[...] = dot(rows_to, raw[:, start : start + cols]).astype(bf16)

    pad_cols(0, p_time_qkv)
    pad_rows(1, p_time_o)
    pad_cols(2, p_read_q)
    pad_cols(3, p_read_kv)
    pad_rows(4, p_read_o)
    pad_cols(5, p_write_q)
    pad_cols(6, p_write_kv)
    pad_rows(7, p_write_o)

    for h in range(parts):
        rows = virt[h].reshape(few * virtuals, width).astype(f32)
        normed = (unit(rows) * gains[4:5, :]).astype(bf16)
        queries = dot(normed, p_read_q[...]).astype(bf16)
        vq[h * few : (h + 1) * few] = queries.reshape(few, virtuals, WIDE)

    flipped = (vis[...].astype(f32) - 1.0) * PENALTY
    read_bias[...] = jnp.concatenate([flipped, flipped], axis=-1)

    each(nfrm, lambda k: vis_copy(k).wait_recv())
    vis_recv[pl.ds(me, 1)] = vis[...][None]
    seen = [vis_recv[s].astype(f32) for s in range(nfrm)]
    seen = [s[h * few : (h + 1) * few] for h in range(parts) for s in seen]
    row = lax.broadcasted_iota(jnp.int32, (owned, tracks), 0)
    col = lax.broadcasted_iota(jnp.int32, (owned, tracks), 1)
    pick = jnp.where(col == row + me * owned, 1.0, 0.0).astype(bf16)
    time_bias[...] = (dot_t(pick, jnp.concatenate(seen, axis=0).astype(bf16)) - 1.0) * PENALTY
    own.wait()

    def project(c, carry):
        each(nfrm, lambda k: tok_copy(c, k).wait_recv())
        rows = []
        for t in range(per):
            blocks = [x_recv[s, c * per + t].astype(f32) for s in range(nfrm)]
            rows += [b[h * few : (h + 1) * few] for h in range(parts) for b in blocks]
        rows = jnp.concatenate(rows, axis=0)
        normed = (unit(rows) * gains[0:1, :]).astype(bf16)
        triple = dot(normed, p_time_qkv[...]).astype(bf16)
        qkv[pl.ds(c * per, per)] = triple.reshape(per, keys, 3 * WIDE)
        return carry

    lax.fori_loop(0, chunks, project, 0)
    asked = keys // parts

    def attend(n):
        h, first = n // 2, n % 2 * batch
        lane_k = lanes(keys)
        blocks = [(t, p) for t in range(batch) for p in range(PAIRS)]
        bias = [time_bias[first + t : first + t + 1, :] for t in range(batch)]
        bias = [jnp.concatenate([b, b], axis=-1) for b in bias]

        def piece(m, t, p):
            cols = slice(m * WIDE + p * TILE, m * WIDE + (p + 1) * TILE)
            if m == 0:
                return qkv[first + t, h * asked : (h + 1) * asked, cols]
            return qkv[first + t, :, cols]

        scores = [dot_t(piece(0, t, p), halves(piece(1, t, p), lane_k)) * SCALE + bias[t] for t, p in blocks]
        heads = [s[:, m * keys : (m + 1) * keys] for s in scores for m in range(2)]
        peaks = [jnp.max(s, axis=-1, keepdims=True) for s in heads]
        expos = [jnp.exp(s - m).astype(bf16) for s, m in zip(heads, peaks)]
        ones = sum_columns(keys)
        sums = [
            dot(
                jnp.concatenate(expos[2 * m : 2 * m + 2], axis=-1),
                jnp.concatenate([halves(piece(2, t, p), lane_k), ones], axis=-1),
            )
            for m, (t, p) in enumerate(blocks)
        ]
        tiles = [(x[:, :TILE] / x[:, TILE:]).astype(bf16) for x in sums]
        outs = [jnp.concatenate(tiles[t * PAIRS : (t + 1) * PAIRS], axis=-1) for t in range(batch)]
        projected = dot(jnp.concatenate(outs, axis=0), p_time_o[...])
        for s in range(nfrm):
            mine = [
                projected[t * asked + s * few : t * asked + (s + 1) * few] for t in range(batch)
            ]
            stage[n, s] = jnp.concatenate(mine, axis=0).astype(bf16)
        if n < 2:
            each(nfrm, lambda k: back_copy(n, k).start())
        y_recv[n, pl.ds(me, 1)] = stage[n, pl.ds(me, 1)]

    for n in range(2 * parts):
        attend(n)

    def send_back(n):
        each(nfrm, lambda k: back_copy(n, k).start())

    def next_part(h):
        for n in (2 * h - 2, 2 * h - 1):
            each(nfrm, lambda k: back_copy(n, k).wait_send())
        send_back(2 * h)
        send_back(2 * h + 1)

    next_part(1)

    def add(h):
        for b in range(2):
            n = h * 2 + b
            each(nfrm, lambda k: back_copy(n, k).wait_recv())
            for o in range(nfrm):
                old = tok[o, b * batch : (b + 1) * batch].astype(f32)[:, h * few : (h + 1) * few]
                total = old + y_recv[n, o].astype(f32).reshape(batch, few, width)
                total = total.astype(bf16).astype(f32).reshape(batch * few, width)
                start = (o * owned + b * batch) * few
                for m in range(width // TILE):
                    y1t[m, start : start + batch * few, :] = total[:, m * TILE : (m + 1) * TILE]
        rows = []
        for f in range(few):
            rows.append(
                jnp.concatenate(
                    [y1t[m, pl.ds(f, tracks, stride=few), :] for m in range(width // TILE)], axis=-1
                )
            )
        rows = jnp.concatenate(rows, axis=0)
        span = slice(h * few, (h + 1) * few)
        y1[span] = rows.astype(bf16).reshape(few, tracks, width)
        normed = (unit(rows) * gains[1:2, :]).astype(bf16)
        kv2[span] = dot(normed, p_read_kv[...]).astype(bf16).reshape(few, tracks, 2 * WIDE)

    def write_queries(h):
        span = slice(h * few, (h + 1) * few)
        rows = y1[span].reshape(few * tracks, width).astype(f32)
        normed = (unit(rows) * gains[2:3, :]).astype(bf16)
        wq[span] = dot(normed, p_write_q[...]).astype(bf16).reshape(few, tracks, WIDE)

    def part_copy(h, i):
        other = lax.rem(spot + i, nplane)
        return remote(
            pay.at[h, other],
            part.at[h, spot],
            (part_sem.at[0, h, i], part_sem.at[1, h, i]),
            (other * 2 + half, me),
        )

    def across(h):
        return remote(
            cross.at[h, half], cross.at[h, half], (cross_sem.at[0, h], cross_sem.at[1, h]), partner
        )

    def gather_copy(h, i):
        return remote(
            vout.at[h, spot],
            vout.at[h, spot],
            (gather_sem.at[0, h, i], gather_sem.at[1, h, i]),
            (lax.rem(spot + i, nplane) * 2 + half, me),
        )

    def read(h):
        at = [p * TILE for p in range(PAIRS)]
        inside = range(h * few, (h + 1) * few)
        nums, dens, peaks = pair_attention(
            [vq[f, :, a : a + TILE] for f in inside for a in at],
            [kv2[f, :, a : a + TILE] for f in inside for a in at],
            [kv2[f, :, WIDE + a : WIDE + a + TILE] for f in inside for a in at],
            [read_bias[f : f + 1, :] for f in inside for a in at],
        )
        tiles = [with_peak(with_den(num, den), peak) for num, den, peak in zip(nums, dens, peaks)]
        for n in range(few):
            rows = jnp.concatenate(tiles[n * PAIRS : (n + 1) * PAIRS], axis=-1)
            for r in range(0, virtuals, unit_rows):
                u = (n * virtuals + r) // unit_rows
                pay[h, u] = rows[r : r + unit_rows]
        each(nplane, lambda i: part_copy(h, i).start())
        part[h, pl.ds(spot, 1)] = pay[h, pl.ds(spot, 1)]

    def cross_step(h):
        each(nplane, lambda i: part_copy(h, i).wait_recv())
        cross[h, pl.ds(half, 1)] = merge_tiles(part[h])[None]
        across(h).start()

    def virtual_step(h):
        across(h).wait_recv()
        both = cross[h]
        readout = jnp.concatenate(
            [over_den(merge(both[:, :, p * TILE : (p + 1) * TILE])[0]) for p in range(PAIRS)], axis=-1
        )
        virt1 = (virt[h, spot].astype(f32) + dot(readout, p_read_o[...])).astype(bf16).astype(f32)
        normed = (unit(virt1) * gains[5:6, :]).astype(bf16)
        middle = gelu(dot(normed, r_vup[...])).astype(bf16)
        vout[h, spot] = (virt1 + dot(middle, r_vdown[...])).astype(bf16)
        each(nplane, lambda i: gather_copy(h, i).start())

    def out_copy(at, group):
        span = pl.ds(at, group)
        return pltpu.make_async_copy(outv.at[span], track_out.at[span], out_sem.at[at])

    def write(h, g, group):
        if g == 0:
            each(nplane, lambda i: gather_copy(h, i).wait_recv())
        units = range(g * virtuals // unit_rows, (g + group) * virtuals // unit_rows)
        rows = jnp.concatenate([vout[h, u] for u in units], axis=0).astype(f32)
        normed = (unit(rows) * gains[6:7, :]).astype(bf16)
        pairs = dot(normed, p_write_kv[...]).astype(bf16)
        span = slice(h * few + g, h * few + g + group)
        at = [p * TILE for p in range(PAIRS)]
        blocks = [pairs[n * virtuals : (n + 1) * virtuals] for n in range(group)]
        nums, dens, _ = pair_attention(
            [wq[f, :, a : a + TILE] for f in range(span.start, span.stop) for a in at],
            [block[:, a : a + TILE] for block in blocks for a in at],
            [block[:, WIDE + a : WIDE + a + TILE] for block in blocks for a in at],
            None,
        )
        tiles = [(num / den).astype(bf16) for num, den in zip(nums, dens)]
        outs = [jnp.concatenate(tiles[n * PAIRS : (n + 1) * PAIRS], axis=-1) for n in range(group)]
        first = y1[span].reshape(group * tracks, width).astype(f32)
        second = first + dot(jnp.concatenate(outs, axis=0), p_write_o[...])
        second = second.astype(bf16).astype(f32)
        normed = (unit(second) * gains[3:4, :]).astype(bf16)
        middle = gelu(dot(normed, r_up[...])).astype(bf16)
        final = second + dot(middle, r_down[...])
        outv[span] = final.astype(bf16).reshape(group, tracks, width)
        out_copy(span.start, group).start()

    written = [(h * few, few) for h in range(parts)]
    add(0)
    read(0)
    next_part(2)
    write_queries(0)
    add(1)
    read(1)
    cross_step(0)
    next_part(3)
    write_queries(1)
    add(2)
    read(2)
    cross_step(1)
    virtual_step(0)
    write_queries(2)
    add(3)
    read(3)
    cross_step(2)
    virtual_step(1)
    write_queries(3)
    write(0, 0, few)
    cross_step(3)
    virtual_step(2)
    write(1, 0, few)
    virtual_step(3)
    write(2, 0, few)
    write(3, 0, few)

    virt_done = pltpu.make_async_copy(vout, virt_out, own_sem)
    virt_done.start()

    each(nfrm, lambda k: vis_copy(k).wait_send())
    for c in range(chunks):
        each(nfrm, lambda k: tok_copy(c, k).wait_send())
    for n in range(2 * parts - 2, 2 * parts):
        each(nfrm, lambda k: back_copy(n, k).wait_send())
    for h in range(parts):
        each(nplane, lambda i: part_copy(h, i).wait_send())
        across(h).wait_send()
        each(nplane, lambda i: gather_copy(h, i).wait_send())
    for start, count in written:
        out_copy(start, count).wait()
    virt_done.wait()


def shards(tokens, visible, virtual, gains, *weights):
    tracks, frames, width = tokens.shape
    nfrm, nplane = lax.axis_size("frm"), lax.axis_size("trk") // 2
    virtuals = virtual.shape[1]
    owned = tracks // nfrm
    chunks, parts = 2, 4
    per = owned // chunks
    few = frames // parts
    unit_rows = few * virtuals // nplane
    hidden = weights[8].shape[1]
    keys = nfrm * frames
    dims = (nfrm, nplane, chunks, per, frames, parts)
    narrow = (nfrm, owned, frames, width)
    shares = (parts, nplane, unit_rows, width)
    vmem, anywhere = pl.BlockSpec(memory_space=pltpu.VMEM), pl.BlockSpec(memory_space=pl.ANY)
    dma = pltpu.SemaphoreType.DMA
    raw_cols = sum(w.shape[1] for w in weights[:8])
    track_out, virt_out = pl.pallas_call(
        functools.partial(kernel, dims),
        out_shape=(
            jax.ShapeDtypeStruct((frames, tracks, width), bf16),
            jax.ShapeDtypeStruct(shares, bf16),
        ),
        in_specs=[anywhere, anywhere, anywhere, vmem] + [anywhere] * 12,
        out_specs=(anywhere, anywhere),
        scratch_shapes=[
            pltpu.VMEM(narrow, bf16),
            pltpu.VMEM(narrow, bf16),
            pltpu.VMEM((owned, keys, 3 * WIDE), bf16),
            pltpu.VMEM((2 * parts, nfrm, owned // 2 * few, width), bf16),
            pltpu.VMEM((2 * parts, nfrm, owned // 2 * few, width), bf16),
            pltpu.VMEM((frames, tracks), jnp.int32),
            pltpu.VMEM((nfrm, frames, tracks), jnp.int32),
            pltpu.VMEM((owned, keys), f32),
            pltpu.VMEM((frames, 2 * tracks), f32),
            pltpu.VMEM((width // TILE, tracks * few, TILE), f32),
            pltpu.VMEM((frames, tracks, width), bf16),
            pltpu.VMEM(shares, bf16),
            pltpu.VMEM((frames, virtuals, WIDE), bf16),
            pltpu.VMEM((frames, tracks, 2 * WIDE), bf16),
            pltpu.VMEM((frames, tracks, WIDE), bf16),
            pltpu.VMEM((parts, nplane, unit_rows, WIDE), bf16),
            pltpu.VMEM((parts, nplane, unit_rows, WIDE), bf16),
            pltpu.VMEM((parts, 2, unit_rows, WIDE), bf16),
            pltpu.VMEM(shares, bf16),
            pltpu.VMEM((frames, tracks, width), bf16),
            pltpu.VMEM((width, raw_cols), bf16),
            pltpu.VMEM((width, hidden), bf16),
            pltpu.VMEM((hidden, width), bf16),
            pltpu.VMEM((width, hidden), bf16),
            pltpu.VMEM((hidden, width), bf16),
            pltpu.VMEM((width, 3 * WIDE), bf16),
            pltpu.VMEM((WIDE, width), bf16),
            pltpu.VMEM((width, WIDE), bf16),
            pltpu.VMEM((width, 2 * WIDE), bf16),
            pltpu.VMEM((WIDE, width), bf16),
            pltpu.VMEM((width, WIDE), bf16),
            pltpu.VMEM((width, 2 * WIDE), bf16),
            pltpu.VMEM((WIDE, width), bf16),
            dma((15,)),
            dma,
            dma((2, nfrm)),
            dma((2, chunks, nfrm)),
            dma((2, 2 * parts, nfrm)),
            dma((2, parts, nplane)),
            dma((2, parts)),
            dma((2, parts, nplane)),
            dma((frames,)),
        ],
        compiler_params=pltpu.CompilerParams(
            collective_id=0, has_side_effects=True, vmem_limit_bytes=56 * 1024 * 1024
        ),
    )(tokens.reshape(narrow), jnp.transpose(visible), virtual.reshape(shares), gains, *weights)
    return jnp.transpose(track_out, (1, 0, 2)), virt_out.reshape(frames, virtuals, width)


def solution(mesh):
    in_specs = (P("trk", "frm", None), P("trk", "frm"), P("frm", None, None)) + (P(),) * 13
    out_specs = (P("trk", "frm", None), P("frm", None, None))
    return jax.shard_map(shards, mesh=mesh, in_specs=in_specs, out_specs=out_specs, check_vma=False)
```
